128 devices in a mesh: passage: 8 (over y_hi, z), list: 16 (over x, y_lo, core).
Axes of the slice: x: 4, y: 4 (y_hi: 2, y_lo: 2; y = y_hi * 2 + y_lo), z: 4, core: 2. Of those that a mesh axis runs over, the one named last changes fastest.
Arguments:
- passages: bfloat16 [65536, 1024], P(('passage', 'list')), may hold values from -6 to 6
- list_ids: int32 [65536], P(('passage', 'list')), may hold values from 0 to 65535, as said below
- old_centroids: float32 [65536, 1024], P(('passage', 'list')), may hold values from -6 to 6
- rotation: float32 [1024, 1024], replicated, may hold values from -0.1875 to 0.1875
Outputs:
- rotated: bfloat16 [65536, 1024], P(('passage', 'list'))
- centroids: float32 [65536, 1024], P(('passage', 'list'))
The draws below stay inside these ranges and needn't reach their ends.
Inputs may be any that keep to these rules, and one draw needn't show every extreme that they name: `list_ids`: on each device the ids of its 512 passages never fall. The lists o * 512 to (o + 1) * 512 - 1 belong to owner o, the device of index o along passage+list. At most 8 passages of one device fall in one owner's lists, and in every draw some owners take exactly 8 from every device.
All inputs are finite; a program needn't handle non-finite values.
Results may differ from the reference program's by a relative error of at most 0.001.
Values may be sent and summed in bfloat16 or wider, within the bound.
A program may use at most 64 MiB of HBM per device.

```python
import jax
import jax.numpy as jnp
from jax import lax

D = 1024
LIST_DEV = 512
PDEV = 512
LISTS = 65536
PASSAGES = 65536
CAPO = 8
N_PASSAGE = 8
N_LIST = 16
DEVICES = 128


def draw_list_ids(key, part):
    key_pair, key_hot, key_cold, key_local = jax.random.split(jax.random.fold_in(key, 11), 4)
    half = N_PASSAGE // 2
    pick = jax.random.randint(key_pair, (DEVICES, half, N_LIST), 0, CAPO + 1)
    paired = jnp.concatenate([pick, CAPO - pick], axis=1)
    hot = jax.random.randint(key_hot, (), 0, N_LIST)
    cold = (hot + 1 + jax.random.randint(key_cold, (DEVICES,), 0, N_LIST - 1)) % N_LIST
    column = jnp.arange(N_LIST, dtype=jnp.int32)[None, None, :]
    loads = jnp.where(column == hot, CAPO, jnp.where(column == cold[:, None, None], 0, paired))
    loads = loads.reshape(DEVICES, DEVICES).astype(jnp.int32)
    ends = jnp.cumsum(loads, axis=1)
    positions = jnp.arange(PDEV, dtype=jnp.int32)
    owner = jnp.sum((positions[None, :, None] >= ends[:, None, :]).astype(jnp.int32), axis=2)
    local = jax.random.randint(key_local, (DEVICES, PDEV), 0, LIST_DEV)
    return jnp.sort(owner * LIST_DEV + local, axis=1).reshape(-1).astype(jnp.int32)


def steps_of(stream_key, shape, shards, smallest, top_value):
    gain = 1.0
    for axis_at, parts in shards:
        steps = jax.random.uniform(jax.random.fold_in(jax.random.fold_in(stream_key, 6), axis_at), (parts,), jnp.float32, smallest / len(shards), top_value / len(shards))
        gain = gain * jnp.repeat(jnp.exp(steps), shape[axis_at] // parts).reshape((-1,) + (1,) * (len(shape) - 1 - axis_at))
    return gain


def centred(key, dims, spread, most, pieces=(), kind=jnp.bfloat16):
    drawn = jax.random.normal(key, dims, jnp.float32) * spread
    if len(pieces) > 0:
        drawn = steps_of(key, dims, pieces, -0.22, 0.18) * drawn
    return jnp.clip(drawn, min=-most, max=most).astype(kind)


def setup_inputs(seed: int = 0) -> dict:
    splits = jax.random.split(jax.random.key(seed), 5)
    return {
        "passages": centred(splits[0], (PASSAGES, D), 1.0, 6.0, ((0, 128),)),
        "list_ids": draw_list_ids(jax.random.fold_in(splits[4], 71), 0),
        "old_centroids": centred(splits[2], (LISTS, D), 1.0, 6.0, ((0, 128),), jnp.float32),
        "rotation": centred(splits[3], (D, D), D ** -0.5, 0.1875, (), jnp.float32),
    }


def reference(passages, list_ids, old_centroids, rotation):
    values = passages.astype(jnp.float32)
    sums = jax.ops.segment_sum(values, list_ids, num_segments=LISTS)
    tally = jax.ops.segment_sum(jnp.ones(list_ids.shape, jnp.float32), list_ids, num_segments=LISTS)
    centroids = (sums + old_centroids) / (tally[:, None] + 1.0)
    residual = values - jnp.take(centroids, list_ids, axis=0)
    rotated = jnp.dot(residual, rotation, preferred_element_type=jnp.float32, precision=lax.Precision.HIGHEST)
    return rotated.astype(jnp.bfloat16), centroids
```

```python
import jax
import jax.numpy as jnp
from jax import lax
from jax.experimental import pallas as pl
from jax.experimental.pallas import tpu as pltpu
from jax.sharding import PartitionSpec as P

NP, NL = 8, 16
DEV = NP * NL
CAP = 8
ROWS = 512
LISTS = 512
D = 1024
BLK = NL * CAP
TILE = 256
MESH = pl.DeviceIdType.MESH
F32, BF16, I32 = jnp.float32, jnp.bfloat16, jnp.int32


def dot(a, b):
    return jnp.dot(a, b, preferred_element_type=F32)


def iota(shape, dim):
    return lax.broadcasted_iota(I32, shape, dim)


def far_first(digit):
    return (2 - digit) + 3 * (digit // 2) - 2 * (digit // 3)


def device_at(x, y, z, core):
    return ((y // 2) * 4 + z, x * 4 + (y % 2) * 2 + core)


def whole(ref, sem):
    pltpu.make_async_copy(ref, ref, sem).wait()


def kernel(
    ids_ref, pass_ref, old_hbm, rot_hbm, out_ref, cent_hbm,
    old, rot, rot_hi, rot_lo, send1, recv1, send2, recv2,
    cent, cent_hi, cent_lo, res_hi, res_lo, member, member_t, unpack,
    id1_s, id1_r, id2_s, id2_r,
    sem_send, sem_recv, sem_id, sem_local, sem_bar,
):
    p, l = lax.axis_index("passage"), lax.axis_index("list")
    me = p * NL + l
    x, y, z = l // 4, (p // 4) * 2 + (l // 2) % 2, p % 4

    barrier = pltpu.get_barrier_semaphore()

    def greet_row(k, _):
        pl.semaphore_signal(barrier, inc=1, device_id=(p, (l + k) % NL), device_id_type=MESH)
        return 0

    def greet_column(k, _):
        pl.semaphore_signal(barrier, inc=1, device_id=((p + k) % NP, l), device_id_type=MESH)
        return 0

    lax.fori_loop(1, NP, greet_column, 0)
    lax.fori_loop(1, NL, greet_row, 0)

    load_old = pltpu.make_async_copy(old_hbm, old, sem_local.at[0])
    load_rot = pltpu.make_async_copy(rot_hbm, rot, sem_local.at[1])
    load_rot.start()
    load_old.start()

    ids_row = ids_ref[...].astype(F32)
    eye = iota((ROWS, ROWS), 0) == iota((ROWS, ROWS), 1)
    ids_col = jnp.sum(jnp.where(eye, ids_row, 0.0), axis=1, keepdims=True)
    own_row = jnp.floor(ids_row * (1.0 / LISTS))
    own_col = jnp.floor(ids_col * (1.0 / LISTS))
    before_row = jnp.sum(jnp.where(own_col < own_row, 1.0, 0.0), axis=0, keepdims=True)
    before_col = jnp.sum(jnp.where(own_row < own_col, 1.0, 0.0), axis=1, keepdims=True)
    slot_row = (own_row * CAP + iota((1, ROWS), 1).astype(F32) - before_row).astype(I32)
    slot_col = (own_col * CAP + iota((ROWS, 1), 0).astype(F32) - before_col).astype(I32)
    mark_col = ids_col - own_col * LISTS + 1.0

    for b in range(NP):
        hit = slot_col == iota((ROWS, BLK), 1) + b * BLK
        id1_s[b] = jnp.sum(jnp.where(hit, mark_col, 0.0), axis=0, keepdims=True).astype(I32)
        unpack[:, b * BLK : (b + 1) * BLK] = jnp.where(hit, 1.0, 0.0).astype(BF16)

    def fill(b, _):
        hit = slot_row == iota((BLK, ROWS), 0) + b * BLK
        rows = dot(jnp.where(hit, 1.0, 0.0).astype(BF16), pass_ref[...])
        send1[pl.ds(b * NL, NL)] = rows.astype(BF16).reshape(NL, CAP, D)
        return 0

    lax.fori_loop(0, NP, fill, 0)

    load_rot.wait()

    def split_rot(i, _):
        s = pl.ds(pl.multiple_of(i * 128, 128), 128)
        full = rot[s, :]
        high = full.astype(BF16)
        rot_hi[s, :] = high
        rot_lo[s, :] = (full - high.astype(F32)).astype(BF16)
        return 0

    lax.fori_loop(0, D // 128, split_rot, 0)

    pl.semaphore_wait(barrier, NP + NL - 2)

    def row_is_in(k, _):
        pl.semaphore_signal(sem_bar, inc=1, device_id=((p + k) % NP, l), device_id_type=MESH)
        return 0

    lax.fori_loop(1, NP, row_is_in, 0)

    def id_hop1(k, _):
        other = (p + k) % NP
        pltpu.make_async_remote_copy(
            src_ref=id1_s.at[other], dst_ref=id1_r.at[p], send_sem=sem_id.at[0], recv_sem=sem_id.at[1],
            device_id=(other, l), device_id_type=MESH,
        ).start()
        return 0

    lax.fori_loop(1, NP, id_hop1, 0)
    pltpu.make_async_copy(id1_s.at[p], id1_r.at[p], sem_id.at[1]).start()
    pl.semaphore_wait(sem_bar, NP - 1)

    def route(k, _):
        core, turn, a, b = k // 64, (k // 16) % 4, (k // 4) % 4, k % 4
        c = (turn + a + b) % 4
        dev = device_at((x + far_first(a)) % 4, (y + far_first(b)) % 4, (z + far_first(c)) % 4, core)
        there = dev[0] * NL + dev[1]

        @pl.when(there != me)
        def _():
            pltpu.make_async_remote_copy(
                src_ref=send1.at[there], dst_ref=recv1.at[me], send_sem=sem_send.at[0], recv_sem=sem_recv.at[0],
                device_id=dev, device_id_type=MESH,
            ).start()

        return 0

    lax.fori_loop(0, DEV // 2, route, 0)
    pltpu.make_async_copy(send1.at[me], recv1.at[me], sem_recv.at[0]).start()

    whole(id1_r, sem_id.at[1])
    lane = iota((NP, BLK), 1)
    mine = (lane >= l * CAP) & (lane < l * CAP + CAP)
    got = id1_r[...].reshape(NP, BLK)
    for k in range(NL):
        turned = pltpu.roll(got, lax.rem(l - k + NL, NL) * CAP, 1)
        id2_s[k] = jnp.where(mine, turned, 0)

    def id_hop2(k, _):
        other = (l + k) % NL
        pltpu.make_async_remote_copy(
            src_ref=id2_s.at[other], dst_ref=id2_r.at[l], send_sem=sem_id.at[2], recv_sem=sem_id.at[3],
            device_id=(p, other), device_id_type=MESH,
        ).start()
        return 0

    lax.fori_loop(1, NL, id_hop2, 0)
    pltpu.make_async_copy(id2_s.at[l], id2_r.at[l], sem_id.at[3]).start()

    lax.fori_loop(DEV // 2, DEV, route, 0)

    whole(id2_r, sem_id.at[3])
    marks = jnp.sum(id2_r[...].astype(F32), axis=0)
    eye = iota((BLK, BLK), 0) == iota((BLK, BLK), 1)
    tally = jnp.zeros((LISTS, 1), F32)
    for b in range(NP):
        row = marks[b : b + 1, :]
        hit = jnp.where(iota((LISTS, BLK), 0) + 1 == row.astype(I32), 1.0, 0.0)
        member[:, b * BLK : (b + 1) * BLK] = hit.astype(BF16)
        tally = tally + jnp.sum(hit, axis=1, keepdims=True)
        col = jnp.sum(jnp.where(eye, row, 0.0), axis=1, keepdims=True).astype(I32)
        hit = jnp.where(iota((BLK, LISTS), 1) + 1 == col, 1.0, 0.0)
        member_t[b * BLK : (b + 1) * BLK, :] = hit.astype(BF16)
    load_old.wait()
    tally = tally + 1.0

    whole(recv1, sem_recv.at[0])
    for n in range(D // TILE):
        s = slice(n * TILE, (n + 1) * TILE)
        sums = dot(member[...], recv1[:, :, s].reshape(DEV * CAP, TILE))
        mean = (sums + old[:, s]) / tally
        high = mean.astype(BF16)
        cent[:, s] = mean
        cent_hi[:, s] = high
        cent_lo[:, s] = (mean - high.astype(F32)).astype(BF16)
    store_cent = pltpu.make_async_copy(cent, cent_hbm, sem_local.at[2])
    store_cent.start()

    def chunk(i, _):
        y_hi = (p // 4 + 1 + i // 2) % 2
        z_a = (z + 2 + i % 2) % 4
        z_b = (z + 1 + 3 * (i % 2)) % 4
        blocks = (y_hi * 4 + z_a, y_hi * 4 + z_b)
        for h, blk in enumerate(blocks):
            half = slice(h * BLK, (h + 1) * BLK)
            pick = member_t[pl.ds(pl.multiple_of(blk * BLK, BLK), BLK), :]
            for n in range(D // TILE):
                s = slice(n * TILE, (n + 1) * TILE)
                near = dot(pick, cent_hi[:, s]) + dot(pick, cent_lo[:, s])
                rows = recv1[pl.ds(blk * NL, NL), :, s].reshape(BLK, TILE).astype(F32)
                res = rows - near
                high = res.astype(BF16)
                res_hi[half, s] = high
                res_lo[half, s] = (res - high.astype(F32)).astype(BF16)
        for n in range(D // TILE):
            s = slice(n * TILE, (n + 1) * TILE)
            turned = dot(res_hi[...], rot_hi[:, s]) + dot(res_hi[...], rot_lo[:, s]) + dot(res_lo[...], rot_hi[:, s])
            turned = turned.astype(BF16)
            for h, blk in enumerate(blocks):
                send2[pl.ds(blk * NL, NL), :, s] = turned[h * BLK : (h + 1) * BLK].reshape(NL, CAP, TILE)

        def give_back(k, _):
            core, h, a, b = k // 16, (k // 8) % 2, (k // 2) % 4, k % 2
            z_to = z_a * (1 - h) + z_b * h
            there_p = y_hi * 4 + z_to
            there_l = ((x + far_first(a)) % 4) * 4 + ((l // 2 + 1 + b) % 2) * 2 + core
            there = there_p * NL + there_l

            @pl.when(there != me)
            def _():
                pltpu.make_async_remote_copy(
                    src_ref=send2.at[there], dst_ref=recv2.at[me], send_sem=sem_send.at[1], recv_sem=sem_recv.at[1],
                    device_id=(there_p, there_l), device_id_type=MESH,
                ).start()

            return 0

        lax.fori_loop(0, 2 * NL, give_back, 0)
        return 0

    lax.fori_loop(0, NP // 2, chunk, 0)
    pltpu.make_async_copy(send2.at[me], recv2.at[me], sem_recv.at[1]).start()

    whole(recv2, sem_recv.at[1])
    for n in range(D // TILE):
        s = slice(n * TILE, (n + 1) * TILE)
        out_ref[:, s] = dot(unpack[...], recv2[:, :, s].reshape(DEV * CAP, TILE)).astype(BF16)

    store_cent.wait()
    whole(send1.at[pl.ds(0, DEV - 1)], sem_send.at[0])
    whole(send2.at[pl.ds(0, DEV - 1)], sem_send.at[1])
    whole(id1_s.at[pl.ds(0, NP - 1)], sem_id.at[0])
    whole(id2_s.at[pl.ds(0, NL - 1)], sem_id.at[2])


def shards(passages, list_ids, old_centroids, rotation):
    vmem = pl.BlockSpec(memory_space=pltpu.VMEM)
    hbm = pl.BlockSpec(memory_space=pl.ANY)
    slots = pltpu.VMEM((DEV, CAP, D), BF16)
    return pl.pallas_call(
        kernel,
        out_shape=(
            jax.ShapeDtypeStruct((ROWS, D), BF16),
            jax.ShapeDtypeStruct((LISTS, D), F32),
        ),
        in_specs=[vmem, vmem, hbm, hbm],
        out_specs=(vmem, hbm),
        scratch_shapes=[
            pltpu.VMEM((LISTS, D), F32),
            pltpu.VMEM((D, D), F32),
            pltpu.VMEM((D, D), BF16),
            pltpu.VMEM((D, D), BF16),
            slots, slots, slots, slots,
            pltpu.VMEM((LISTS, D), F32),
            pltpu.VMEM((LISTS, D), BF16),
            pltpu.VMEM((LISTS, D), BF16),
            pltpu.VMEM((2 * BLK, D), BF16),
            pltpu.VMEM((2 * BLK, D), BF16),
            pltpu.VMEM((LISTS, DEV * CAP), BF16),
            pltpu.VMEM((DEV * CAP, LISTS), BF16),
            pltpu.VMEM((ROWS, DEV * CAP), BF16),
            pltpu.VMEM((NP, 1, BLK), I32),
            pltpu.VMEM((NP, 1, BLK), I32),
            pltpu.VMEM((NL, NP, BLK), I32),
            pltpu.VMEM((NL, NP, BLK), I32),
            pltpu.SemaphoreType.DMA((2,)),
            pltpu.SemaphoreType.DMA((2,)),
            pltpu.SemaphoreType.DMA((4,)),
            pltpu.SemaphoreType.DMA((3,)),
            pltpu.SemaphoreType.REGULAR,
        ],
        compiler_params=pltpu.CompilerParams(
            collective_id=0, has_side_effects=True, vmem_limit_bytes=48 << 20
        ),
        cost_estimate=pl.CostEstimate(flops=14 << 30, bytes_accessed=10 << 20, transcendentals=0),
    )(list_ids.reshape(1, ROWS), passages, old_centroids, rotation)


def solution(mesh):
    split = P(("passage", "list"), None)
    return jax.shard_map(
        shards,
        mesh=mesh,
        in_specs=(split, P(("passage", "list")), split, P()),
        out_specs=(split, split),
        check_vma=False,
    )
```

```python
import jax
import jax.numpy as jnp
from jax import lax
from jax.experimental import pallas as pl
from jax.experimental.pallas import tpu as pltpu
from jax.sharding import PartitionSpec as P

NP, NL = 8, 16
DEV = NP * NL
CAP = 8
ROWS = 512
LISTS = 512
D = 1024
BLK = NL * CAP
TILE = 256
MESH = pl.DeviceIdType.MESH
F32, BF16, I32 = jnp.float32, jnp.bfloat16, jnp.int32


def dot(a, b):
    return jnp.dot(a, b, preferred_element_type=F32)


def iota(shape, dim):
    return lax.broadcasted_iota(I32, shape, dim)


def wrap(v, n):
    return jnp.where(v >= n, v - n, v)


def steps(offset):
    return sum(min(d, 4 - d) for d in offset)


OFFSETS = sorted(((a, b, c) for a in range(4) for b in range(4) for c in range(4)), key=steps, reverse=True)
HERE = (0, 0, 0)


class Place:
    def __init__(self):
        self.p, self.l = lax.axis_index("passage"), lax.axis_index("list")
        x, self.y_hi = lax.div(self.l, 4), lax.div(self.p, 4)
        z, rest = self.p - 4 * self.y_hi, self.l - 4 * x
        self.y_lo = lax.div(rest, 2)
        self.core = rest - 2 * self.y_lo
        y = 2 * self.y_hi + self.y_lo
        ys = [wrap(y + d, 4) for d in range(4)]
        self.x_part = [4 * wrap(x + d, 4) for d in range(4)]
        self.z_part = [wrap(z + d, 4) for d in range(4)]
        self.hi_part = [jnp.where(v >= 2, 4, 0) for v in ys]
        self.lo_part = [2 * (v - jnp.where(v >= 2, 2, 0)) for v in ys]
        self.me = self.p * NL + self.l

    def at(self, offset, core):
        a, b, c = offset
        return (self.hi_part[b] + self.z_part[c], self.x_part[a] + self.lo_part[b] + core)


def whole(ref, sem):
    pltpu.make_async_copy(ref, ref, sem).wait()


def signal(sem, device):
    pl.semaphore_signal(sem, inc=1, device_id=device, device_id_type=MESH)


def kernel(
    ids_hbm, pass_hbm, old_hbm, rot_hbm, recv2, cent_out, unpack_out,
    ids_ref, pass_ref, old, rot, rot_hi, rot_lo, send1, recv1, send2,
    cent, cent_hi, cent_lo, res_hi, res_lo, member, member_t, unpack,
    id1_s, id1_r, id2_s, id2_r,
    sem_send, sem_recv, sem_id, sem_local, sem_bar,
):
    at = Place()
    p, l, me = at.p, at.l, at.me

    load_ids = pltpu.make_async_copy(ids_hbm, ids_ref, sem_local.at[0])
    load_pass = pltpu.make_async_copy(pass_hbm, pass_ref, sem_local.at[1])
    load_rot = pltpu.make_async_copy(rot_hbm, rot, sem_local.at[2])
    load_old = pltpu.make_async_copy(old_hbm, old, sem_local.at[3])
    load_ids.start()
    load_pass.start()

    barrier = pltpu.get_barrier_semaphore()
    plane = [(0, b, c) for b in (2, 1, 3, 0) for c in (2, 1, 3, 0) if (b, c) != (0, 0)]
    line = [(a, 0, 0) for a in (2, 1, 3)]
    for offset in plane:
        signal(barrier, at.at(offset, at.core))
    for offset in line:
        for core in range(2):
            signal(barrier, at.at(offset, core))
    signal(barrier, at.at(HERE, 1 - at.core))
    load_rot.start()
    load_old.start()

    load_ids.wait()
    ids_row = ids_ref[...].astype(F32)
    eye = iota((ROWS, ROWS), 0) == iota((ROWS, ROWS), 1)
    ids_col = jnp.sum(jnp.where(eye, ids_row, 0.0), axis=1, keepdims=True)
    own_row = jnp.floor(ids_row * (1.0 / LISTS))
    own_col = jnp.floor(ids_col * (1.0 / LISTS))
    before_row = jnp.sum(jnp.where(own_col < own_row, 1.0, 0.0), axis=0, keepdims=True)
    slot_row = (own_row * CAP + iota((1, ROWS), 1).astype(F32) - before_row).astype(I32)

    load_pass.wait()

    def fill(b, _):
        hit = slot_row == iota((BLK, ROWS), 0) + b * BLK
        rows = dot(jnp.where(hit, 1.0, 0.0).astype(BF16), pass_ref[...])
        send1[pl.ds(b * NL, NL)] = rows.astype(BF16).reshape(NL, CAP, D)
        return 0

    lax.fori_loop(0, NP, fill, 0)

    def route(offset, core):
        device = at.at(offset, core)
        pltpu.make_async_remote_copy(
            src_ref=send1.at[device[0] * NL + device[1]], dst_ref=recv1.at[me],
            send_sem=sem_send.at[0], recv_sem=sem_recv.at[0], device_id=device, device_id_type=MESH,
        ).start()

    pl.semaphore_wait(barrier, len(plane) + 2 * len(line) + 1)
    for offset in plane:
        signal(sem_bar, at.at(offset, at.core))
    for offset in plane:
        route(offset, at.core)
    for offset in line:
        for core in range(2):
            route(offset, core)
    route(HERE, 1 - at.core)
    pltpu.make_async_copy(send1.at[me], recv1.at[me], sem_recv.at[0]).start()

    before_col = jnp.sum(jnp.where(own_row < own_col, 1.0, 0.0), axis=1, keepdims=True)
    slot_col = (own_col * CAP + iota((ROWS, 1), 0).astype(F32) - before_col).astype(I32)
    mark_col = ids_col - own_col * LISTS + 1.0
    for b in range(NP):
        hit = slot_col == iota((ROWS, BLK), 1) + b * BLK
        id1_s[b] = jnp.sum(jnp.where(hit, mark_col, 0.0), axis=0, keepdims=True).astype(I32)
        unpack[:, b * BLK : (b + 1) * BLK] = jnp.where(hit, 1.0, 0.0).astype(BF16)
    for b in (2, 0):
        for c in (2, 1, 3, 0):
            if (b, c) != (0, 0):
                device = at.at((0, b, c), at.core)
                pltpu.make_async_remote_copy(
                    src_ref=id1_s.at[device[0]], dst_ref=id1_r.at[p], send_sem=sem_id.at[0], recv_sem=sem_id.at[1],
                    device_id=device, device_id_type=MESH,
                ).start()
    pltpu.make_async_copy(id1_s.at[p], id1_r.at[p], sem_id.at[1]).start()
    store_unpack = pltpu.make_async_copy(unpack, unpack_out, sem_local.at[0])
    store_unpack.start()
    pl.semaphore_wait(sem_bar, len(plane))

    others = [offset for offset in OFFSETS if offset[0] != 0 and offset[1:] != (0, 0)]

    def route_all(core):
        for offset in others:
            route(offset, core)

        @pl.when(at.core != core)
        def _():
            for offset in plane:
                route(offset, core)

    route_all(0)

    whole(id1_r, sem_id.at[1])
    lane = iota((NP, BLK), 1)
    mine = (lane >= l * CAP) & (lane < l * CAP + CAP)
    got = id1_r[...].reshape(NP, BLK)
    for k in range(NL):
        id2_s[k] = jnp.where(mine, pltpu.roll(got, CAP * wrap(l - k + NL, NL), 1), 0)
    for k in range(1, NL):
        other = wrap(l + k, NL)
        pltpu.make_async_remote_copy(
            src_ref=id2_s.at[other], dst_ref=id2_r.at[l], send_sem=sem_id.at[2], recv_sem=sem_id.at[3],
            device_id=(p, other), device_id_type=MESH,
        ).start()
    pltpu.make_async_copy(id2_s.at[l], id2_r.at[l], sem_id.at[3]).start()

    route_all(1)

    load_rot.wait()

    def split_rot(i, _):
        s = pl.ds(pl.multiple_of(i * 128, 128), 128)
        full = rot[s, :]
        high = full.astype(BF16)
        rot_hi[s, :] = high
        rot_lo[s, :] = (full - high.astype(F32)).astype(BF16)
        return 0

    lax.fori_loop(0, D // 128, split_rot, 0)

    whole(id2_r, sem_id.at[3])
    marks = jnp.sum(id2_r[...].astype(F32), axis=0)
    eye = iota((BLK, BLK), 0) == iota((BLK, BLK), 1)
    tally = jnp.zeros((LISTS, 1), F32)
    for b in range(NP):
        row = marks[b : b + 1, :]
        hit = jnp.where(iota((LISTS, BLK), 0) + 1 == row.astype(I32), 1.0, 0.0)
        member[:, b * BLK : (b + 1) * BLK] = hit.astype(BF16)
        tally = tally + jnp.sum(hit, axis=1, keepdims=True)
        col = jnp.sum(jnp.where(eye, row, 0.0), axis=1, keepdims=True).astype(I32)
        hit = jnp.where(iota((BLK, LISTS), 1) + 1 == col, 1.0, 0.0)
        member_t[b * BLK : (b + 1) * BLK, :] = hit.astype(BF16)
    load_old.wait()
    tally = tally + 1.0

    whole(recv1, sem_recv.at[0])
    for n in range(D // TILE):
        s = slice(n * TILE, (n + 1) * TILE)
        sums = dot(member[...], recv1[:, :, s].reshape(DEV * CAP, TILE))
        mean = (sums + old[:, s]) / tally
        high = mean.astype(BF16)
        cent[:, s] = mean
        cent_hi[:, s] = high
        cent_lo[:, s] = (mean - high.astype(F32)).astype(BF16)
    store_cent = pltpu.make_async_copy(cent, cent_out, sem_local.at[1])
    store_cent.start()

    def chunk(i, _):
        far = lax.div(i, 2)
        flip = i - 2 * far
        y_hi = wrap(at.y_hi + 1 + far, 2)
        y_hi = wrap(y_hi, 2)
        z_a = wrap(at.z_part[0] + 2 + flip, 4)
        z_b = wrap(at.z_part[0] + 1 + 3 * flip, 4)
        z_b = wrap(z_b, 4)
        blocks = (y_hi * 4 + z_a, y_hi * 4 + z_b)
        for h, blk in enumerate(blocks):
            half = slice(h * BLK, (h + 1) * BLK)
            pick = member_t[pl.ds(pl.multiple_of(blk * BLK, BLK), BLK), :]
            for n in range(D // TILE):
                s = slice(n * TILE, (n + 1) * TILE)
                near = dot(pick, cent_hi[:, s]) + dot(pick, cent_lo[:, s])
                rows = recv1[pl.ds(blk * NL, NL), :, s].reshape(BLK, TILE).astype(F32)
                res = rows - near
                high = res.astype(BF16)
                res_hi[half, s] = high
                res_lo[half, s] = (res - high.astype(F32)).astype(BF16)
        for n in range(D // TILE):
            s = slice(n * TILE, (n + 1) * TILE)
            turned = dot(res_hi[...], rot_hi[:, s]) + dot(res_hi[...], rot_lo[:, s]) + dot(res_lo[...], rot_hi[:, s])
            turned = turned.astype(BF16)
            for h, blk in enumerate(blocks):
                send2[pl.ds(blk * NL, NL), :, s] = turned[h * BLK : (h + 1) * BLK].reshape(NL, CAP, TILE)

        def give_back(there_p, there_l):
            pltpu.make_async_remote_copy(
                src_ref=send2.at[there_p * NL + there_l], dst_ref=recv2.at[me],
                send_sem=sem_send.at[1], recv_sem=sem_recv.at[1],
                device_id=(there_p, there_l), device_id_type=MESH,
            ).start()

        for core in range(2):
            for blk in blocks:
                for a in (2, 1, 3, 0):
                    for lo in (2 - 2 * at.y_lo, 2 * at.y_lo):
                        there_l = at.x_part[a] + lo + core
                        if a == 0 and blk is blocks[1]:

                            @pl.when((blk != p) | (there_l != l))
                            def _():
                                give_back(blk, there_l)
                        else:
                            give_back(blk, there_l)
        return 0

    lax.fori_loop(0, NP // 2, chunk, 0)
    pltpu.make_async_copy(send2.at[me], recv2.at[me], sem_recv.at[1]).start()

    whole(send1.at[pl.ds(0, DEV - 1)], sem_send.at[0])
    whole(id1_s.at[pl.ds(0, NP - 1)], sem_id.at[0])
    whole(id2_s.at[pl.ds(0, NL - 1)], sem_id.at[2])
    store_unpack.wait()
    store_cent.wait()
    whole(send2.at[pl.ds(0, DEV - 1)], sem_send.at[1])
    whole(recv2, sem_recv.at[1])


def finish(unpack, rows, cent, out, cent_out, buf, sem):
    store = pltpu.make_async_copy(cent, cent_out, sem.at[D // TILE])
    store.start()
    stores = []
    for n in range(D // TILE):
        s = pl.ds(n * TILE, TILE)
        buf[:, s] = dot(unpack[...], rows[:, :, s].reshape(DEV * CAP, TILE)).astype(BF16)
        stores.append(pltpu.make_async_copy(buf.at[:, s], out.at[:, s], sem.at[n]))
        stores[-1].start()
    for copy in (store, *stores):
        copy.wait()


def shards(passages, list_ids, old_centroids, rotation):
    vmem = pl.BlockSpec(memory_space=pltpu.VMEM)
    hbm = pl.BlockSpec(memory_space=pl.ANY)
    slots = jax.ShapeDtypeStruct((DEV, CAP, D), BF16)
    buffer = pltpu.VMEM((DEV, CAP, D), BF16)
    means = jax.ShapeDtypeStruct((LISTS, D), F32)
    arrays = (list_ids.reshape(1, ROWS), passages, old_centroids, rotation)
    rows, cent, unpack = pl.pallas_call(
        kernel,
        out_shape=(slots, means, jax.ShapeDtypeStruct((ROWS, DEV * CAP), BF16)),
        in_specs=[hbm] * 4,
        out_specs=(hbm,) * 3,
        scratch_shapes=[
            pltpu.VMEM((1, ROWS), I32),
            pltpu.VMEM((ROWS, D), BF16),
            pltpu.VMEM((LISTS, D), F32),
            pltpu.VMEM((D, D), F32),
            pltpu.VMEM((D, D), BF16),
            pltpu.VMEM((D, D), BF16),
            buffer, buffer, buffer,
            pltpu.VMEM((LISTS, D), F32),
            pltpu.VMEM((LISTS, D), BF16),
            pltpu.VMEM((LISTS, D), BF16),
            pltpu.VMEM((2 * BLK, D), BF16),
            pltpu.VMEM((2 * BLK, D), BF16),
            pltpu.VMEM((LISTS, DEV * CAP), BF16),
            pltpu.VMEM((DEV * CAP, LISTS), BF16),
            pltpu.VMEM((ROWS, DEV * CAP), BF16),
            pltpu.VMEM((NP, 1, BLK), I32),
            pltpu.VMEM((NP, 1, BLK), I32),
            pltpu.VMEM((NL, NP, BLK), I32),
            pltpu.VMEM((NL, NP, BLK), I32),
            pltpu.SemaphoreType.DMA((2,)),
            pltpu.SemaphoreType.DMA((2,)),
            pltpu.SemaphoreType.DMA((4,)),
            pltpu.SemaphoreType.DMA((4,)),
            pltpu.SemaphoreType.REGULAR,
        ],
        compiler_params=pltpu.CompilerParams(
            collective_id=0, has_side_effects=True, vmem_limit_bytes=36 << 20
        ),
        cost_estimate=pl.CostEstimate(flops=14 << 30, bytes_accessed=10 << 20, transcendentals=0),
    )(*(pltpu.with_memory_space_constraint(a, pltpu.HBM) for a in arrays))
    return pl.pallas_call(
        finish,
        out_shape=(jax.ShapeDtypeStruct((ROWS, D), BF16), means),
        in_specs=[vmem, vmem, hbm],
        out_specs=(hbm, hbm),
        scratch_shapes=[pltpu.VMEM((ROWS, D), BF16), pltpu.SemaphoreType.DMA((D // TILE + 1,))],
        compiler_params=pltpu.CompilerParams(vmem_limit_bytes=16 << 20),
        cost_estimate=pl.CostEstimate(flops=1 << 30, bytes_accessed=9 << 20, transcendentals=0),
    )(unpack, rows, cent)


def solution(mesh):
    split = P(("passage", "list"), None)
    return jax.shard_map(
        shards,
        mesh=mesh,
        in_specs=(split, P(("passage", "list")), split, P()),
        out_specs=(split, split),
        check_vma=False,
    )
```

```python
import random

import jax
import jax.numpy as jnp
from jax import lax
from jax.experimental import pallas as pl
from jax.experimental.pallas import tpu as pltpu
from jax.sharding import PartitionSpec as P

NP, NL = 8, 16
DEV = NP * NL
CAP = 8
ROWS = 512
LISTS = 512
D = 1024
BLK = NL * CAP
TILE = 256
PARTS = 4
PACK = 512
CHUNK = 32
MESH = pl.DeviceIdType.MESH
F32, BF16, I32 = jnp.float32, jnp.bfloat16, jnp.int32


def dot(a, b):
    return jnp.dot(a, b, preferred_element_type=F32)


def iota(shape, dim):
    return lax.broadcasted_iota(I32, shape, dim)


def wrap(v, n):
    return jnp.where(v >= n, v - n, v)


def steps(offset):
    return sum(min(d, 4 - d) for d in offset)


def send_order(seed):
    offsets = [(a, b, c) for a in range(4) for b in range(4) for c in range(4)]
    random.Random(seed).shuffle(offsets)
    return sorted(offsets, key=steps, reverse=True)


OFFSETS = send_order(3)
CHIPS = len(OFFSETS)
HERE = (0, 0, 0)


def seen_from_there(offset):
    return OFFSETS.index(tuple((4 - d) % 4 for d in offset))


class Place:
    def __init__(self):
        self.p, self.l = lax.axis_index("passage"), lax.axis_index("list")
        x, self.y_hi = lax.div(self.l, 4), lax.div(self.p, 4)
        z, rest = self.p - 4 * self.y_hi, self.l - 4 * x
        self.y_lo = lax.div(rest, 2)
        self.core = rest - 2 * self.y_lo
        y = 2 * self.y_hi + self.y_lo
        ys = [wrap(y + d, 4) for d in range(4)]
        self.x_part = [4 * wrap(x + d, 4) for d in range(4)]
        self.z_part = [wrap(z + d, 4) for d in range(4)]
        self.hi_part = [jnp.where(v >= 2, 4, 0) for v in ys]
        self.lo_part = [2 * (v - jnp.where(v >= 2, 2, 0)) for v in ys]
        self.me = self.p * NL + self.l

    def at(self, offset, core):
        a, b, c = offset
        return (self.hi_part[b] + self.z_part[c], self.x_part[a] + self.lo_part[b] + core)


def whole(ref, sem):
    pltpu.make_async_copy(ref, ref, sem).wait()


def signal(sem, device):
    pl.semaphore_signal(sem, inc=1, device_id=device, device_id_type=MESH)


def kernel(
    ids_hbm, pass_hbm, old_hbm, rot_hbm, recv2, cent_out, unpack_out,
    ids_ref, pass_ref, old, rot, rot_hi, rot_lo, send1, recv1, send2,
    cent, cent_hi, cent_lo, res_hi, res_lo, member, member_t, unpack,
    id1_s, id1_r, id2_s, id2_r,
    sem_send, sem_recv, sem_id, sem_local, sem_bar,
):
    at = Place()
    p, l, me = at.p, at.l, at.me

    load_ids = pltpu.make_async_copy(ids_hbm, ids_ref, sem_local.at[0])
    load_pass = pltpu.make_async_copy(pass_hbm, pass_ref, sem_local.at[1])
    load_rot = pltpu.make_async_copy(rot_hbm, rot, sem_local.at[2])
    load_old = pltpu.make_async_copy(old_hbm, old, sem_local.at[3])
    load_ids.start()
    load_pass.start()

    barrier = pltpu.get_barrier_semaphore()
    plane = [(0, b, c) for b in (2, 1, 3, 0) for c in (2, 1, 3, 0) if (b, c) != (0, 0)]
    line = [(a, 0, 0) for a in (2, 1, 3)]
    for offset in plane:
        signal(barrier, at.at(offset, at.core))
    for offset in line:
        for core in range(2):
            signal(barrier, at.at(offset, core))
    signal(barrier, at.at(HERE, 1 - at.core))
    load_rot.start()
    load_old.start()

    load_ids.wait()
    ids_row = ids_ref[...].astype(F32)
    eye = iota((ROWS, ROWS), 0) == iota((ROWS, ROWS), 1)
    ids_col = jnp.sum(jnp.where(eye, ids_row, 0.0), axis=1, keepdims=True)
    own_row = jnp.floor(ids_row * (1.0 / LISTS))
    own_col = jnp.floor(ids_col * (1.0 / LISTS))
    before_row = jnp.sum(jnp.where(own_col < own_row, 1.0, 0.0), axis=0, keepdims=True)
    slot_row = (own_row * CAP + iota((1, ROWS), 1).astype(F32) - before_row).astype(I32)

    load_pass.wait()

    def fill(b, _):
        hit = slot_row == iota((PACK, ROWS), 0) + b * PACK
        hit = jnp.where(hit, 1.0, 0.0).astype(BF16)
        at_b = pl.ds(b * (PACK // CAP), PACK // CAP)
        for n in range(D // TILE):
            cols = slice(n * TILE, (n + 1) * TILE)
            send1[at_b, :, cols] = dot(hit, pass_ref[:, cols]).astype(BF16).reshape(PACK // CAP, CAP, TILE)
        return 0

    lax.fori_loop(0, DEV * CAP // PACK, fill, 0)

    def route(offset, core):
        device = at.at(offset, core)
        pltpu.make_async_remote_copy(
            src_ref=send1.at[device[0] * NL + device[1]], dst_ref=recv1.at[at.core * CHIPS + seen_from_there(offset)],
            send_sem=sem_send.at[0], recv_sem=sem_recv.at[0], device_id=device, device_id_type=MESH,
        ).start()

    pl.semaphore_wait(barrier, len(plane) + 2 * len(line) + 1)
    for offset in plane:
        signal(sem_bar, at.at(offset, at.core))
    for offset in plane:
        route(offset, at.core)
    for offset in line:
        for core in range(2):
            route(offset, core)
    route(HERE, 1 - at.core)
    pltpu.make_async_copy(send1.at[me], recv1.at[at.core * CHIPS + OFFSETS.index(HERE)], sem_recv.at[0]).start()

    before_col = jnp.sum(jnp.where(own_row < own_col, 1.0, 0.0), axis=1, keepdims=True)
    slot_col = (own_col * CAP + iota((ROWS, 1), 0).astype(F32) - before_col).astype(I32)
    mark_col = ids_col - own_col * LISTS + 1.0
    for b in range(NP):
        hit = slot_col == iota((ROWS, BLK), 1) + b * BLK
        id1_s[b] = jnp.sum(jnp.where(hit, mark_col, 0.0), axis=0, keepdims=True).astype(I32)
        unpack[:, b * BLK : (b + 1) * BLK] = jnp.where(hit, 1.0, 0.0).astype(BF16)
    for b in (2, 0):
        for c in (2, 1, 3, 0):
            if (b, c) != (0, 0):
                device = at.at((0, b, c), at.core)
                pltpu.make_async_remote_copy(
                    src_ref=id1_s.at[device[0]], dst_ref=id1_r.at[p], send_sem=sem_id.at[0], recv_sem=sem_id.at[1],
                    device_id=device, device_id_type=MESH,
                ).start()
    pltpu.make_async_copy(id1_s.at[p], id1_r.at[p], sem_id.at[1]).start()
    store_unpack = pltpu.make_async_copy(unpack, unpack_out, sem_local.at[0])
    store_unpack.start()
    pl.semaphore_wait(sem_bar, len(plane))

    others = [offset for offset in OFFSETS if offset[0] != 0 and offset[1:] != (0, 0)]

    def route_all(core):
        for offset in others:
            route(offset, core)

        @pl.when(at.core != core)
        def _():
            for offset in plane:
                route(offset, core)

    route_all(0)

    whole(id1_r, sem_id.at[1])
    source = iota((NP, BLK), 1) // CAP
    got = id1_r[...].reshape(NP, BLK)
    for k in range(NL):
        spread = jnp.where(source == k, got, 0)
        for turn in (CAP, 2 * CAP, 4 * CAP, 8 * CAP):
            spread = spread + pltpu.roll(spread, turn, 1)
        id2_s[k] = spread
    for k in range(1, NL):
        other = wrap(l + k, NL)
        pltpu.make_async_remote_copy(
            src_ref=id2_s.at[other], dst_ref=id2_r.at[l], send_sem=sem_id.at[2], recv_sem=sem_id.at[3],
            device_id=(p, other), device_id_type=MESH,
        ).start()
    pltpu.make_async_copy(id2_s.at[l], id2_r.at[l], sem_id.at[3]).start()

    route_all(1)

    load_rot.wait()

    def split_rot(i, _):
        s = pl.ds(pl.multiple_of(i * 128, 128), 128)
        full = rot[s, :]
        high = full.astype(BF16)
        rot_hi[s, :] = high
        rot_lo[s, :] = (full - high.astype(F32)).astype(BF16)
        return 0

    lax.fori_loop(0, D // 128, split_rot, 0)

    whole(id2_r, sem_id.at[3])
    row_of = jnp.zeros((CHIPS, 1), I32)
    for k, offset in enumerate(OFFSETS):
        there_p, there_l = at.at(offset, 0)
        row_of = jnp.where(iota((CHIPS, 1), 0) == k, there_l * NP + there_p, row_of)
    here = iota((CHIPS, DEV), 1)
    order = jnp.concatenate([here == row_of, here == row_of + NP], axis=0)
    order = jnp.where(order, 1.0, 0.0).astype(BF16)
    marks = id2_r[...].reshape(DEV, BLK).astype(F32)
    high = jnp.floor(marks * (1.0 / 16))
    marks = dot(order, high.astype(BF16)) * 16.0 + dot(order, (marks - high * 16.0).astype(BF16))
    marks = jnp.where(iota((DEV, BLK), 0) % NL == iota((DEV, BLK), 1) // CAP, marks, 0.0)
    eye = iota((BLK, BLK), 0) == iota((BLK, BLK), 1)
    tally = jnp.zeros((LISTS, 1), F32)
    for b in range(NP):
        row = jnp.sum(marks[b * NL : (b + 1) * NL, :], axis=0, keepdims=True)
        hit = jnp.where(iota((LISTS, BLK), 0) + 1 == row.astype(I32), 1.0, 0.0)
        member[:, b * BLK : (b + 1) * BLK] = hit.astype(BF16)
        tally = tally + jnp.sum(hit, axis=1, keepdims=True)
        col = jnp.sum(jnp.where(eye, row, 0.0), axis=1, keepdims=True).astype(I32)
        hit = jnp.where(iota((BLK, LISTS), 1) + 1 == col, 1.0, 0.0)
        member_t[b * BLK : (b + 1) * BLK, :] = hit.astype(BF16)
    load_old.wait()
    tally = tally + 1.0

    whole(recv1, sem_recv.at[0])
    for n in range(D // TILE):
        s = slice(n * TILE, (n + 1) * TILE)
        sums = dot(member[...], recv1[:, :, s].reshape(DEV * CAP, TILE))
        mean = (sums + old[:, s]) / tally
        high = mean.astype(BF16)
        cent[:, s] = mean
        cent_hi[:, s] = high
        cent_lo[:, s] = (mean - high.astype(F32)).astype(BF16)
    store_cent = pltpu.make_async_copy(cent, cent_out, sem_local.at[1])
    store_cent.start()

    for first in range(0, DEV, CHUNK):
        here = slice(first, first + CHUNK)
        pick = member_t[first * CAP : (first + CHUNK) * CAP, :]
        for n in range(D // TILE):
            s = slice(n * TILE, (n + 1) * TILE)
            near = dot(pick, cent_hi[:, s]) + dot(pick, cent_lo[:, s])
            res = recv1[here, :, s].reshape(CHUNK * CAP, TILE).astype(F32) - near
            high = res.astype(BF16)
            res_hi[:, s] = high
            res_lo[:, s] = (res - high.astype(F32)).astype(BF16)
        for n in range(D // TILE):
            s = slice(n * TILE, (n + 1) * TILE)
            turned = dot(res_hi[...], rot_hi[:, s]) + dot(res_hi[...], rot_lo[:, s]) + dot(res_lo[...], rot_hi[:, s])
            send2[here, :, s] = turned.astype(BF16).reshape(CHUNK, CAP, TILE)

        for k in range(first, first + CHUNK):
            core, offset = k // CHIPS, OFFSETS[k % CHIPS]

            def give_back():
                pltpu.make_async_remote_copy(
                    src_ref=send2.at[k], dst_ref=recv2.at[me], send_sem=sem_send.at[1], recv_sem=sem_recv.at[1],
                    device_id=at.at(offset, core), device_id_type=MESH,
                ).start()

            if offset == HERE:
                pl.when(at.core != core)(give_back)
            else:
                give_back()

    mine = send2.at[at.core * CHIPS + OFFSETS.index(HERE)]
    pltpu.make_async_copy(mine, recv2.at[me], sem_recv.at[1]).start()

    whole(send1.at[pl.ds(0, DEV - 1)], sem_send.at[0])
    whole(id1_s.at[pl.ds(0, NP - 1)], sem_id.at[0])
    whole(id2_s.at[pl.ds(0, NL - 1)], sem_id.at[2])
    store_unpack.wait()
    store_cent.wait()
    whole(send2.at[pl.ds(0, DEV - 1)], sem_send.at[1])
    whole(recv2, sem_recv.at[1])


def finish(unpack, rows, cent, out, cent_out, buf, sem):
    stores = []

    def store(src, dst):
        stores.append(pltpu.make_async_copy(src, dst, sem.at[len(stores)]))
        stores[-1].start()

    for n in range(PARTS):
        rows_n = pl.ds(n * (LISTS // PARTS), LISTS // PARTS)
        store(cent.at[rows_n], cent_out.at[rows_n])
    for n in range(PARTS):
        rows_n = pl.ds(n * (ROWS // PARTS), ROWS // PARTS)
        buf[rows_n] = dot(unpack[rows_n], rows[...].reshape(DEV * CAP, D)).astype(BF16)
        store(buf.at[rows_n], out.at[rows_n])
    for copy in stores:
        copy.wait()


def shards(passages, list_ids, old_centroids, rotation):
    vmem = pl.BlockSpec(memory_space=pltpu.VMEM)
    hbm = pl.BlockSpec(memory_space=pl.ANY)
    slots = jax.ShapeDtypeStruct((DEV, CAP, D), BF16)
    buffer = pltpu.VMEM((DEV, CAP, D), BF16)
    means = jax.ShapeDtypeStruct((LISTS, D), F32)
    arrays = (list_ids.reshape(1, ROWS), passages, old_centroids, rotation)
    rows, cent, unpack = pl.pallas_call(
        kernel,
        out_shape=(slots, means, jax.ShapeDtypeStruct((ROWS, DEV * CAP), BF16)),
        in_specs=[hbm] * 4,
        out_specs=(hbm,) * 3,
        scratch_shapes=[
            pltpu.VMEM((1, ROWS), I32),
            pltpu.VMEM((ROWS, D), BF16),
            pltpu.VMEM((LISTS, D), F32),
            pltpu.VMEM((D, D), F32),
            pltpu.VMEM((D, D), BF16),
            pltpu.VMEM((D, D), BF16),
            buffer, buffer, buffer,
            pltpu.VMEM((LISTS, D), F32),
            pltpu.VMEM((LISTS, D), BF16),
            pltpu.VMEM((LISTS, D), BF16),
            pltpu.VMEM((CHUNK * CAP, D), BF16),
            pltpu.VMEM((CHUNK * CAP, D), BF16),
            pltpu.VMEM((LISTS, DEV * CAP), BF16),
            pltpu.VMEM((DEV * CAP, LISTS), BF16),
            pltpu.VMEM((ROWS, DEV * CAP), BF16),
            pltpu.VMEM((NP, 1, BLK), I32),
            pltpu.VMEM((NP, 1, BLK), I32),
            pltpu.VMEM((NL, NP, BLK), I32),
            pltpu.VMEM((NL, NP, BLK), I32),
            pltpu.SemaphoreType.DMA((2,)),
            pltpu.SemaphoreType.DMA((2,)),
            pltpu.SemaphoreType.DMA((4,)),
            pltpu.SemaphoreType.DMA((4,)),
            pltpu.SemaphoreType.REGULAR,
        ],
        compiler_params=pltpu.CompilerParams(
            collective_id=0, has_side_effects=True, vmem_limit_bytes=36 << 20
        ),
        cost_estimate=pl.CostEstimate(flops=14 << 30, bytes_accessed=10 << 20, transcendentals=0),
    )(*(pltpu.with_memory_space_constraint(a, pltpu.HBM) for a in arrays))
    return pl.pallas_call(
        finish,
        out_shape=(jax.ShapeDtypeStruct((ROWS, D), BF16), means),
        in_specs=[vmem, vmem, hbm],
        out_specs=(hbm, hbm),
        scratch_shapes=[pltpu.VMEM((ROWS, D), BF16), pltpu.SemaphoreType.DMA((2 * PARTS,))],
        compiler_params=pltpu.CompilerParams(vmem_limit_bytes=16 << 20),
        cost_estimate=pl.CostEstimate(flops=1 << 30, bytes_accessed=9 << 20, transcendentals=0),
    )(unpack, rows, cent)


def solution(mesh):
    split = P(("passage", "list"), None)
    return jax.shard_map(
        shards,
        mesh=mesh,
        in_specs=(split, P(("passage", "list")), split, P()),
        out_specs=(split, split),
        check_vma=False,
    )
```

```python
import random

import jax
import jax.numpy as jnp
from jax import lax
from jax.experimental import pallas as pl
from jax.experimental.pallas import tpu as pltpu
from jax.sharding import PartitionSpec as P

NP, NL = 8, 16
DEV = NP * NL
CAP = 8
ROWS = 512
LISTS = 512
D = 1024
BLK = NL * CAP
TILE = 256
PARTS = 4
PACK = 512
CHUNKS = (16, 16, 32, 32, 32)
WIDE = 256
MESH = pl.DeviceIdType.MESH
F32, BF16, I32 = jnp.float32, jnp.bfloat16, jnp.int32


def dot(a, b):
    return jnp.dot(a, b, preferred_element_type=F32)


def iota(shape, dim):
    return lax.broadcasted_iota(I32, shape, dim)


def wrap(v, n):
    return jnp.where(v >= n, v - n, v)


def steps(offset):
    return sum(min(d, 4 - d) for d in offset)


def send_order(seed):
    offsets = [(a, b, c) for a in range(4) for b in range(4) for c in range(4)]
    random.Random(seed).shuffle(offsets)
    return sorted(offsets, key=steps, reverse=True)


OFFSETS = send_order(3)
CHIPS = len(OFFSETS)
HERE = (0, 0, 0)


def seen_from_there(offset):
    return OFFSETS.index(tuple((4 - d) % 4 for d in offset))


class Place:
    def __init__(self):
        self.p, self.l = lax.axis_index("passage"), lax.axis_index("list")
        x, self.y_hi = lax.div(self.l, 4), lax.div(self.p, 4)
        z, rest = self.p - 4 * self.y_hi, self.l - 4 * x
        self.y_lo = lax.div(rest, 2)
        self.core = rest - 2 * self.y_lo
        y = 2 * self.y_hi + self.y_lo
        ys = [wrap(y + d, 4) for d in range(4)]
        self.x_part = [4 * wrap(x + d, 4) for d in range(4)]
        self.z_part = [wrap(z + d, 4) for d in range(4)]
        self.hi_part = [jnp.where(v >= 2, 4, 0) for v in ys]
        self.lo_part = [2 * (v - jnp.where(v >= 2, 2, 0)) for v in ys]
        self.me = self.p * NL + self.l

    def at(self, offset, core):
        a, b, c = offset
        return (self.hi_part[b] + self.z_part[c], self.x_part[a] + self.lo_part[b] + core)


def whole(ref, sem):
    pltpu.make_async_copy(ref, ref, sem).wait()


def signal(sem, device):
    pl.semaphore_signal(sem, inc=1, device_id=device, device_id_type=MESH)


def kernel(
    ids_hbm, pass_hbm, old_hbm, rot_hbm, recv2, cent_out, unpack_out,
    ids_ref, pass_ref, old, rot, rot_hi, rot_lo, send1, recv1, send2,
    cent, cent_hi, cent_lo, res, member, member_t, unpack,
    id1_s, id1_r, id2_s, id2_r,
    sem_send, sem_recv, sem_id, sem_local, sem_bar,
):
    at = Place()
    p, l, me = at.p, at.l, at.me

    load_ids = pltpu.make_async_copy(ids_hbm, ids_ref, sem_local.at[0])
    load_pass = pltpu.make_async_copy(pass_hbm, pass_ref, sem_local.at[1])
    load_rot = pltpu.make_async_copy(rot_hbm, rot, sem_local.at[2])
    load_old = pltpu.make_async_copy(old_hbm, old, sem_local.at[3])
    load_ids.start()
    load_pass.start()

    barrier = pltpu.get_barrier_semaphore()
    plane = [(0, b, c) for b in (2, 1, 3, 0) for c in (2, 1, 3, 0) if (b, c) != (0, 0)]
    line = [(a, 0, 0) for a in (2, 1, 3)]
    for offset in plane:
        signal(barrier, at.at(offset, at.core))
    for offset in line:
        for core in range(2):
            signal(barrier, at.at(offset, core))
    signal(barrier, at.at(HERE, 1 - at.core))
    load_rot.start()
    load_old.start()

    load_ids.wait()
    ids_row = ids_ref[...].astype(F32)
    eye = iota((ROWS, ROWS), 0) == iota((ROWS, ROWS), 1)
    ids_col = jnp.sum(jnp.where(eye, ids_row, 0.0), axis=1, keepdims=True)
    own_row = jnp.floor(ids_row * (1.0 / LISTS))
    own_col = jnp.floor(ids_col * (1.0 / LISTS))
    before_row = jnp.sum(jnp.where(own_col < own_row, 1.0, 0.0), axis=0, keepdims=True)
    slot_row = (own_row * CAP + iota((1, ROWS), 1).astype(F32) - before_row).astype(I32)

    load_pass.wait()

    def fill(b, _):
        hit = slot_row == iota((PACK, ROWS), 0) + b * PACK
        hit = jnp.where(hit, 1.0, 0.0).astype(BF16)
        at_b = pl.ds(b * (PACK // CAP), PACK // CAP)
        for n in range(D // TILE):
            cols = slice(n * TILE, (n + 1) * TILE)
            send1[at_b, :, cols] = dot(hit, pass_ref[:, cols]).astype(BF16).reshape(PACK // CAP, CAP, TILE)
        return 0

    lax.fori_loop(0, DEV * CAP // PACK, fill, 0)

    def route(offset, core):
        device = at.at(offset, core)
        pltpu.make_async_remote_copy(
            src_ref=send1.at[device[0] * NL + device[1]], dst_ref=recv1.at[at.core * CHIPS + seen_from_there(offset)],
            send_sem=sem_send.at[0], recv_sem=sem_recv.at[0], device_id=device, device_id_type=MESH,
        ).start()

    pl.semaphore_wait(barrier, len(plane) + 2 * len(line) + 1)
    for offset in plane:
        signal(sem_bar, at.at(offset, at.core))
    for offset in plane:
        route(offset, at.core)
    for offset in line:
        for core in range(2):
            route(offset, core)
    route(HERE, 1 - at.core)
    pltpu.make_async_copy(send1.at[me], recv1.at[at.core * CHIPS + OFFSETS.index(HERE)], sem_recv.at[0]).start()

    before_col = jnp.sum(jnp.where(own_row < own_col, 1.0, 0.0), axis=1, keepdims=True)
    slot_col = (own_col * CAP + iota((ROWS, 1), 0).astype(F32) - before_col).astype(I32)
    mark_col = ids_col - own_col * LISTS + 1.0
    for b in range(NP):
        hit = slot_col == iota((ROWS, BLK), 1) + b * BLK
        id1_s[b] = jnp.sum(jnp.where(hit, mark_col, 0.0), axis=0, keepdims=True).astype(I32)
        unpack[:, b * BLK : (b + 1) * BLK] = jnp.where(hit, 1.0, 0.0).astype(BF16)
    for b in (2, 0):
        for c in (2, 1, 3, 0):
            if (b, c) != (0, 0):
                device = at.at((0, b, c), at.core)
                pltpu.make_async_remote_copy(
                    src_ref=id1_s.at[device[0]], dst_ref=id1_r.at[p], send_sem=sem_id.at[0], recv_sem=sem_id.at[1],
                    device_id=device, device_id_type=MESH,
                ).start()
    pltpu.make_async_copy(id1_s.at[p], id1_r.at[p], sem_id.at[1]).start()
    store_unpack = pltpu.make_async_copy(unpack, unpack_out, sem_local.at[0])
    store_unpack.start()
    pl.semaphore_wait(sem_bar, len(plane))

    others = [offset for offset in OFFSETS if offset[0] != 0 and offset[1:] != (0, 0)]

    def route_all(core):
        for offset in others:
            route(offset, core)

        @pl.when(at.core != core)
        def _():
            for offset in plane:
                route(offset, core)

    route_all(0)

    whole(id1_r, sem_id.at[1])
    source = iota((NP, BLK), 1) // CAP
    got = id1_r[...].reshape(NP, BLK)
    for k in range(NL):
        spread = jnp.where(source == k, got, 0)
        for turn in (CAP, 2 * CAP, 4 * CAP, 8 * CAP):
            spread = spread + pltpu.roll(spread, turn, 1)
        id2_s[k] = spread
    for k in range(1, NL):
        other = wrap(l + k, NL)
        pltpu.make_async_remote_copy(
            src_ref=id2_s.at[other], dst_ref=id2_r.at[l], send_sem=sem_id.at[2], recv_sem=sem_id.at[3],
            device_id=(p, other), device_id_type=MESH,
        ).start()
    pltpu.make_async_copy(id2_s.at[l], id2_r.at[l], sem_id.at[3]).start()

    route_all(1)

    load_rot.wait()

    def split_rot(i, _):
        s = pl.ds(pl.multiple_of(i * 128, 128), 128)
        full = rot[s, :]
        high = full.astype(BF16)
        rot_hi[s, :] = high
        rot_lo[s, :] = (full - high.astype(F32)).astype(BF16)
        return 0

    lax.fori_loop(0, D // 128, split_rot, 0)

    whole(id2_r, sem_id.at[3])
    row_of = jnp.zeros((CHIPS, 1), I32)
    for k, offset in enumerate(OFFSETS):
        there_p, there_l = at.at(offset, 0)
        row_of = jnp.where(iota((CHIPS, 1), 0) == k, there_l * NP + there_p, row_of)
    here = iota((CHIPS, DEV), 1)
    order = jnp.concatenate([here == row_of, here == row_of + NP], axis=0)
    order = jnp.where(order, 1.0, 0.0).astype(BF16)
    marks = id2_r[...].reshape(DEV, BLK).astype(F32)
    high = jnp.floor(marks * (1.0 / 16))
    marks = dot(order, high.astype(BF16)) * 16.0 + dot(order, (marks - high * 16.0).astype(BF16))
    marks = jnp.where(iota((DEV, BLK), 0) % NL == iota((DEV, BLK), 1) // CAP, marks, 0.0)
    eye = iota((BLK, BLK), 0) == iota((BLK, BLK), 1)
    tally = jnp.zeros((LISTS, 1), F32)
    for b in range(NP):
        row = jnp.sum(marks[b * NL : (b + 1) * NL, :], axis=0, keepdims=True)
        hit = jnp.where(iota((LISTS, BLK), 0) + 1 == row.astype(I32), 1.0, 0.0)
        member[:, b * BLK : (b + 1) * BLK] = hit.astype(BF16)
        tally = tally + jnp.sum(hit, axis=1, keepdims=True)
        col = jnp.sum(jnp.where(eye, row, 0.0), axis=1, keepdims=True).astype(I32)
        hit = jnp.where(iota((BLK, LISTS), 1) + 1 == col, 1.0, 0.0)
        member_t[b * BLK : (b + 1) * BLK, :] = hit.astype(BF16)
    load_old.wait()
    tally = tally + 1.0

    whole(recv1, sem_recv.at[0])
    for n in range(D // TILE):
        s = slice(n * TILE, (n + 1) * TILE)
        sums = dot(member[...], recv1[:, :, s].reshape(DEV * CAP, TILE))
        mean = (sums + old[:, s]) / tally
        high = mean.astype(BF16)
        cent[:, s] = mean
        cent_hi[:, s] = high
        cent_lo[:, s] = (mean - high.astype(F32)).astype(BF16)
    store_cent = pltpu.make_async_copy(cent, cent_out, sem_local.at[1])
    store_cent.start()

    first = 0
    for count in CHUNKS:
        here = slice(first, first + count)
        rows = count * CAP
        pick = member_t[first * CAP : first * CAP + rows, :]
        for n in range(D // WIDE):
            s = slice(n * WIDE, (n + 1) * WIDE)
            near = dot(pick, cent_hi[:, s]) + dot(pick, cent_lo[:, s])
            part = recv1[here, :, s].reshape(rows, WIDE).astype(F32) - near
            high = part.astype(BF16)
            res[:rows, s] = high
            res[rows : 2 * rows, s] = (part - high.astype(F32)).astype(BF16)
        for n in range(D // WIDE):
            s = slice(n * WIDE, (n + 1) * WIDE)
            both = dot(res[: 2 * rows], rot_hi[:, s])
            turned = both[:rows] + both[rows:] + dot(res[:rows], rot_lo[:, s])
            send2[here, :, s] = turned.astype(BF16).reshape(count, CAP, WIDE)

        for k in range(first, first + count):
            core, offset = k // CHIPS, OFFSETS[k % CHIPS]

            def give_back():
                pltpu.make_async_remote_copy(
                    src_ref=send2.at[k], dst_ref=recv2.at[me], send_sem=sem_send.at[1], recv_sem=sem_recv.at[1],
                    device_id=at.at(offset, core), device_id_type=MESH,
                ).start()

            if offset == HERE:
                pl.when(at.core != core)(give_back)
            else:
                give_back()
        first += count

    mine = send2.at[at.core * CHIPS + OFFSETS.index(HERE)]
    pltpu.make_async_copy(mine, recv2.at[me], sem_recv.at[1]).start()

    whole(send1.at[pl.ds(0, DEV - 1)], sem_send.at[0])
    whole(id1_s.at[pl.ds(0, NP - 1)], sem_id.at[0])
    whole(id2_s.at[pl.ds(0, NL - 1)], sem_id.at[2])
    store_unpack.wait()
    store_cent.wait()
    whole(send2.at[pl.ds(0, DEV - 1)], sem_send.at[1])
    whole(recv2, sem_recv.at[1])


def finish(unpack, rows, cent, out, cent_out, buf, sem):
    stores = []

    def store(src, dst):
        stores.append(pltpu.make_async_copy(src, dst, sem.at[len(stores)]))
        stores[-1].start()

    for n in range(PARTS):
        rows_n = pl.ds(n * (LISTS // PARTS), LISTS // PARTS)
        store(cent.at[rows_n], cent_out.at[rows_n])
    for n in range(PARTS):
        rows_n = pl.ds(n * (ROWS // PARTS), ROWS // PARTS)
        buf[rows_n] = dot(unpack[rows_n], rows[...].reshape(DEV * CAP, D)).astype(BF16)
        store(buf.at[rows_n], out.at[rows_n])
    for copy in stores:
        copy.wait()


def shards(passages, list_ids, old_centroids, rotation):
    vmem = pl.BlockSpec(memory_space=pltpu.VMEM)
    hbm = pl.BlockSpec(memory_space=pl.ANY)
    slots = jax.ShapeDtypeStruct((DEV, CAP, D), BF16)
    buffer = pltpu.VMEM((DEV, CAP, D), BF16)
    means = jax.ShapeDtypeStruct((LISTS, D), F32)
    arrays = (list_ids.reshape(1, ROWS), passages, old_centroids, rotation)
    rows, cent, unpack = pl.pallas_call(
        kernel,
        out_shape=(slots, means, jax.ShapeDtypeStruct((ROWS, DEV * CAP), BF16)),
        in_specs=[hbm] * 4,
        out_specs=(hbm,) * 3,
        scratch_shapes=[
            pltpu.VMEM((1, ROWS), I32),
            pltpu.VMEM((ROWS, D), BF16),
            pltpu.VMEM((LISTS, D), F32),
            pltpu.VMEM((D, D), F32),
            pltpu.VMEM((D, D), BF16),
            pltpu.VMEM((D, D), BF16),
            buffer, buffer, buffer,
            pltpu.VMEM((LISTS, D), F32),
            pltpu.VMEM((LISTS, D), BF16),
            pltpu.VMEM((LISTS, D), BF16),
            pltpu.VMEM((2 * max(CHUNKS) * CAP, D), BF16),
            pltpu.VMEM((LISTS, DEV * CAP), BF16),
            pltpu.VMEM((DEV * CAP, LISTS), BF16),
            pltpu.VMEM((ROWS, DEV * CAP), BF16),
            pltpu.VMEM((NP, 1, BLK), I32),
            pltpu.VMEM((NP, 1, BLK), I32),
            pltpu.VMEM((NL, NP, BLK), I32),
            pltpu.VMEM((NL, NP, BLK), I32),
            pltpu.SemaphoreType.DMA((2,)),
            pltpu.SemaphoreType.DMA((2,)),
            pltpu.SemaphoreType.DMA((4,)),
            pltpu.SemaphoreType.DMA((4,)),
            pltpu.SemaphoreType.REGULAR,
        ],
        compiler_params=pltpu.CompilerParams(
            collective_id=0, has_side_effects=True, vmem_limit_bytes=36 << 20
        ),
        cost_estimate=pl.CostEstimate(flops=14 << 30, bytes_accessed=10 << 20, transcendentals=0),
    )(*(pltpu.with_memory_space_constraint(a, pltpu.HBM) for a in arrays))
    return pl.pallas_call(
        finish,
        out_shape=(jax.ShapeDtypeStruct((ROWS, D), BF16), means),
        in_specs=[vmem, vmem, hbm],
        out_specs=(hbm, hbm),
        scratch_shapes=[pltpu.VMEM((ROWS, D), BF16), pltpu.SemaphoreType.DMA((2 * PARTS,))],
        compiler_params=pltpu.CompilerParams(vmem_limit_bytes=16 << 20),
        cost_estimate=pl.CostEstimate(flops=1 << 30, bytes_accessed=9 << 20, transcendentals=0),
    )(unpack, rows, cent)


def solution(mesh):
    split = P(("passage", "list"), None)
    return jax.shard_map(
        shards,
        mesh=mesh,
        in_specs=(split, P(("passage", "list")), split, P()),
        out_specs=(split, split),
        check_vma=False,
    )
```

```python
import random

import jax
import jax.numpy as jnp
from jax import lax
from jax.experimental import pallas as pl
from jax.experimental.pallas import tpu as pltpu
from jax.sharding import PartitionSpec as P

NP, NL = 8, 16
DEV = NP * NL
CAP = 8
ROWS = 512
LISTS = 512
D = 1024
BLK = NL * CAP
TILE = 256
PARTS = 4
PACK = 512
CHUNKS = (16, 16, 32, 32, 32)
WIDE = 256
MESH = pl.DeviceIdType.MESH
F32, BF16, I32 = jnp.float32, jnp.bfloat16, jnp.int32


def dot(a, b):
    return jnp.dot(a, b, preferred_element_type=F32)


def iota(shape, dim):
    return lax.broadcasted_iota(I32, shape, dim)


def wrap(v, n):
    return jnp.where(v >= n, v - n, v)


def steps(offset):
    return sum(min(d, 4 - d) for d in offset)


def send_order(seed):
    offsets = [(a, b, c) for a in range(4) for b in range(4) for c in range(4)]
    random.Random(seed).shuffle(offsets)
    return sorted(offsets, key=steps, reverse=True)


OFFSETS = send_order(3)
CHIPS = len(OFFSETS)
HERE = (0, 0, 0)


def seen_from_there(offset):
    return OFFSETS.index(tuple((4 - d) % 4 for d in offset))


class Place:
    def __init__(self):
        self.p, self.l = lax.axis_index("passage"), lax.axis_index("list")
        x, self.y_hi = lax.div(self.l, 4), lax.div(self.p, 4)
        z, rest = self.p - 4 * self.y_hi, self.l - 4 * x
        self.y_lo = lax.div(rest, 2)
        self.core = rest - 2 * self.y_lo
        y = 2 * self.y_hi + self.y_lo
        ys = [wrap(y + d, 4) for d in range(4)]
        self.x_part = [4 * wrap(x + d, 4) for d in range(4)]
        self.z_part = [wrap(z + d, 4) for d in range(4)]
        self.hi_part = [jnp.where(v >= 2, 4, 0) for v in ys]
        self.lo_part = [2 * (v - jnp.where(v >= 2, 2, 0)) for v in ys]
        self.me = self.p * NL + self.l

    def at(self, offset, core):
        a, b, c = offset
        return (self.hi_part[b] + self.z_part[c], self.x_part[a] + self.lo_part[b] + core)


def whole(ref, sem):
    pltpu.make_async_copy(ref, ref, sem).wait()


def signal(sem, device):
    pl.semaphore_signal(sem, inc=1, device_id=device, device_id_type=MESH)


def kernel(
    ids_hbm, pass_hbm, old_hbm, rot_hbm, recv2, cent_out, unpack_out,
    ids_ref, pass_ref, old, rot, rot_hi, rot_lo, send1, recv1, send2,
    cent, cent_hi, cent_lo, res, member, member_t, unpack,
    id1_s, id1_r, id2_s, id2_r,
    sem_send, sem_recv, sem_id, sem_local, sem_bar,
):
    at = Place()
    p, l, me = at.p, at.l, at.me

    load_ids = pltpu.make_async_copy(ids_hbm, ids_ref, sem_local.at[0])
    load_pass = pltpu.make_async_copy(pass_hbm, pass_ref, sem_local.at[1])
    load_rot = pltpu.make_async_copy(rot_hbm, rot, sem_local.at[2])
    load_old = pltpu.make_async_copy(old_hbm, old, sem_local.at[3])
    load_ids.start()
    load_pass.start()

    barrier = pltpu.get_barrier_semaphore()
    plane = [(0, b, c) for b in (2, 1, 3, 0) for c in (2, 1, 3, 0) if (b, c) != (0, 0)]
    line = [(a, 0, 0) for a in (2, 1, 3)]
    for offset in plane:
        signal(barrier, at.at(offset, at.core))
    for offset in line:
        for core in range(2):
            signal(barrier, at.at(offset, core))
    signal(barrier, at.at(HERE, 1 - at.core))
    load_rot.start()
    load_old.start()

    load_ids.wait()
    ids_row = ids_ref[...].astype(F32)
    eye = iota((ROWS, ROWS), 0) == iota((ROWS, ROWS), 1)
    ids_col = jnp.sum(jnp.where(eye, ids_row, 0.0), axis=1, keepdims=True)
    own_row = jnp.floor(ids_row * (1.0 / LISTS))
    own_col = jnp.floor(ids_col * (1.0 / LISTS))
    before_row = jnp.sum(jnp.where(own_col < own_row, 1.0, 0.0), axis=0, keepdims=True)
    slot_row = (own_row * CAP + iota((1, ROWS), 1).astype(F32) - before_row).astype(I32)

    load_pass.wait()

    def fill(b, _):
        hit = slot_row == iota((PACK, ROWS), 0) + b * PACK
        hit = jnp.where(hit, 1.0, 0.0).astype(BF16)
        at_b = pl.ds(b * (PACK // CAP), PACK // CAP)
        for n in range(D // TILE):
            cols = slice(n * TILE, (n + 1) * TILE)
            send1[at_b, :, cols] = dot(hit, pass_ref[:, cols]).astype(BF16).reshape(PACK // CAP, CAP, TILE)
        return 0

    lax.fori_loop(0, DEV * CAP // PACK, fill, 0)

    def route(offset, core):
        device = at.at(offset, core)
        pltpu.make_async_remote_copy(
            src_ref=send1.at[device[0] * NL + device[1]], dst_ref=recv1.at[(1 - at.core) * CHIPS + seen_from_there(offset)],
            send_sem=sem_send.at[0], recv_sem=sem_recv.at[0], device_id=device, device_id_type=MESH,
        ).start()

    pl.semaphore_wait(barrier, len(plane) + 2 * len(line) + 1)
    for offset in plane:
        signal(sem_bar, at.at(offset, at.core))
    for offset in plane:
        route(offset, at.core)
    for offset in line:
        for core in range(2):
            route(offset, core)
    route(HERE, 1 - at.core)
    pltpu.make_async_copy(send1.at[me], recv1.at[(1 - at.core) * CHIPS + OFFSETS.index(HERE)], sem_recv.at[0]).start()

    before_col = jnp.sum(jnp.where(own_row < own_col, 1.0, 0.0), axis=1, keepdims=True)
    slot_col = (own_col * CAP + iota((ROWS, 1), 0).astype(F32) - before_col).astype(I32)
    mark_col = ids_col - own_col * LISTS + 1.0
    for b in range(NP):
        hit = slot_col == iota((ROWS, BLK), 1) + b * BLK
        id1_s[b] = jnp.sum(jnp.where(hit, mark_col, 0.0), axis=0, keepdims=True).astype(I32)
        unpack[:, b * BLK : (b + 1) * BLK] = jnp.where(hit, 1.0, 0.0).astype(BF16)
    for b in (2, 0):
        for c in (2, 1, 3, 0):
            if (b, c) != (0, 0):
                device = at.at((0, b, c), at.core)
                pltpu.make_async_remote_copy(
                    src_ref=id1_s.at[device[0]], dst_ref=id1_r.at[p], send_sem=sem_id.at[0], recv_sem=sem_id.at[1],
                    device_id=device, device_id_type=MESH,
                ).start()
    pltpu.make_async_copy(id1_s.at[p], id1_r.at[p], sem_id.at[1]).start()
    store_unpack = pltpu.make_async_copy(unpack, unpack_out, sem_local.at[0])
    store_unpack.start()
    pl.semaphore_wait(sem_bar, len(plane))

    others = [offset for offset in OFFSETS if offset[0] != 0 and offset[1:] != (0, 0)]

    def route_all(core):
        for offset in others:
            route(offset, core)

        @pl.when(at.core != core)
        def _():
            for offset in plane:
                route(offset, core)

    route_all(0)

    whole(id1_r, sem_id.at[1])
    source = iota((NP, BLK), 1) // CAP
    got = id1_r[...].reshape(NP, BLK)
    for k in range(NL):
        spread = jnp.where(source == k, got, 0)
        for turn in (CAP, 2 * CAP, 4 * CAP, 8 * CAP):
            spread = spread + pltpu.roll(spread, turn, 1)
        id2_s[k] = spread
    for k in range(1, NL):
        other = wrap(l + k, NL)
        pltpu.make_async_remote_copy(
            src_ref=id2_s.at[other], dst_ref=id2_r.at[l], send_sem=sem_id.at[2], recv_sem=sem_id.at[3],
            device_id=(p, other), device_id_type=MESH,
        ).start()
    pltpu.make_async_copy(id2_s.at[l], id2_r.at[l], sem_id.at[3]).start()

    route_all(1)

    load_rot.wait()

    def split_rot(i, _):
        s = pl.ds(pl.multiple_of(i * 128, 128), 128)
        full = rot[s, :]
        high = full.astype(BF16)
        rot_hi[s, :] = high
        rot_lo[s, :] = (full - high.astype(F32)).astype(BF16)
        return 0

    lax.fori_loop(0, D // 128, split_rot, 0)

    whole(id2_r, sem_id.at[3])
    row_of = jnp.zeros((CHIPS, 1), I32)
    for k, offset in enumerate(OFFSETS):
        there_p, there_l = at.at(offset, 0)
        row_of = jnp.where(iota((CHIPS, 1), 0) == k, there_l * NP + there_p, row_of)
    here = iota((CHIPS, DEV), 1)
    order = jnp.concatenate([here == row_of + NP, here == row_of], axis=0)
    order = jnp.where(order, 1.0, 0.0).astype(BF16)
    marks = id2_r[...].reshape(DEV, BLK).astype(F32)
    high = jnp.floor(marks * (1.0 / 16))
    marks = dot(order, high.astype(BF16)) * 16.0 + dot(order, (marks - high * 16.0).astype(BF16))
    marks = jnp.where(iota((DEV, BLK), 0) % NL == iota((DEV, BLK), 1) // CAP, marks, 0.0)
    eye = iota((BLK, BLK), 0) == iota((BLK, BLK), 1)
    tally = jnp.zeros((LISTS, 1), F32)
    for b in range(NP):
        row = jnp.sum(marks[b * NL : (b + 1) * NL, :], axis=0, keepdims=True)
        hit = jnp.where(iota((LISTS, BLK), 0) + 1 == row.astype(I32), 1.0, 0.0)
        member[:, b * BLK : (b + 1) * BLK] = hit.astype(BF16)
        tally = tally + jnp.sum(hit, axis=1, keepdims=True)
        col = jnp.sum(jnp.where(eye, row, 0.0), axis=1, keepdims=True).astype(I32)
        hit = jnp.where(iota((BLK, LISTS), 1) + 1 == col, 1.0, 0.0)
        member_t[b * BLK : (b + 1) * BLK, :] = hit.astype(BF16)
    load_old.wait()
    tally = tally + 1.0

    whole(recv1, sem_recv.at[0])
    for n in range(D // TILE):
        s = slice(n * TILE, (n + 1) * TILE)
        sums = dot(member[...], recv1[:, :, s].reshape(DEV * CAP, TILE))
        mean = (sums + old[:, s]) / tally
        high = mean.astype(BF16)
        cent[:, s] = mean
        cent_hi[:, s] = high
        cent_lo[:, s] = (mean - high.astype(F32)).astype(BF16)
    store_cent = pltpu.make_async_copy(cent, cent_out, sem_local.at[1])
    store_cent.start()

    first = 0
    for count in CHUNKS:
        here = slice(first, first + count)
        rows = count * CAP
        pick = member_t[first * CAP : first * CAP + rows, :]
        for n in range(D // WIDE):
            s = slice(n * WIDE, (n + 1) * WIDE)
            near = dot(pick, cent_hi[:, s]) + dot(pick, cent_lo[:, s])
            part = recv1[here, :, s].reshape(rows, WIDE).astype(F32) - near
            high = part.astype(BF16)
            res[:rows, s] = high
            res[rows : 2 * rows, s] = (part - high.astype(F32)).astype(BF16)
        for n in range(D // WIDE):
            s = slice(n * WIDE, (n + 1) * WIDE)
            both = dot(res[: 2 * rows], rot_hi[:, s])
            turned = both[:rows] + both[rows:] + dot(res[:rows], rot_lo[:, s])
            send2[here, :, s] = turned.astype(BF16).reshape(count, CAP, WIDE)

        for k in range(first, first + count):
            core, offset = 1 - k // CHIPS, OFFSETS[k % CHIPS]

            def give_back():
                pltpu.make_async_remote_copy(
                    src_ref=send2.at[k], dst_ref=recv2.at[me], send_sem=sem_send.at[1], recv_sem=sem_recv.at[1],
                    device_id=at.at(offset, core), device_id_type=MESH,
                ).start()

            if offset == HERE:
                pl.when(at.core != core)(give_back)
            else:
                give_back()
        first += count

    mine = send2.at[(1 - at.core) * CHIPS + OFFSETS.index(HERE)]
    pltpu.make_async_copy(mine, recv2.at[me], sem_recv.at[1]).start()

    whole(send1.at[pl.ds(0, DEV - 1)], sem_send.at[0])
    whole(id1_s.at[pl.ds(0, NP - 1)], sem_id.at[0])
    whole(id2_s.at[pl.ds(0, NL - 1)], sem_id.at[2])
    store_unpack.wait()
    store_cent.wait()
    whole(send2.at[pl.ds(0, DEV - 1)], sem_send.at[1])
    whole(recv2, sem_recv.at[1])


def finish(unpack, rows, cent, out, cent_out, buf, sem):
    stores = []

    def store(src, dst):
        stores.append(pltpu.make_async_copy(src, dst, sem.at[len(stores)]))
        stores[-1].start()

    for n in range(PARTS):
        rows_n = pl.ds(n * (LISTS // PARTS), LISTS // PARTS)
        store(cent.at[rows_n], cent_out.at[rows_n])
    for n in range(PARTS):
        rows_n = pl.ds(n * (ROWS // PARTS), ROWS // PARTS)
        buf[rows_n] = dot(unpack[rows_n], rows[...].reshape(DEV * CAP, D)).astype(BF16)
        store(buf.at[rows_n], out.at[rows_n])
    for copy in stores:
        copy.wait()


def shards(passages, list_ids, old_centroids, rotation):
    vmem = pl.BlockSpec(memory_space=pltpu.VMEM)
    hbm = pl.BlockSpec(memory_space=pl.ANY)
    slots = jax.ShapeDtypeStruct((DEV, CAP, D), BF16)
    buffer = pltpu.VMEM((DEV, CAP, D), BF16)
    means = jax.ShapeDtypeStruct((LISTS, D), F32)
    arrays = (list_ids.reshape(1, ROWS), passages, old_centroids, rotation)
    rows, cent, unpack = pl.pallas_call(
        kernel,
        out_shape=(slots, means, jax.ShapeDtypeStruct((ROWS, DEV * CAP), BF16)),
        in_specs=[hbm] * 4,
        out_specs=(hbm,) * 3,
        scratch_shapes=[
            pltpu.VMEM((1, ROWS), I32),
            pltpu.VMEM((ROWS, D), BF16),
            pltpu.VMEM((LISTS, D), F32),
            pltpu.VMEM((D, D), F32),
            pltpu.VMEM((D, D), BF16),
            pltpu.VMEM((D, D), BF16),
            buffer, buffer, buffer,
            pltpu.VMEM((LISTS, D), F32),
            pltpu.VMEM((LISTS, D), BF16),
            pltpu.VMEM((LISTS, D), BF16),
            pltpu.VMEM((2 * max(CHUNKS) * CAP, D), BF16),
            pltpu.VMEM((LISTS, DEV * CAP), BF16),
            pltpu.VMEM((DEV * CAP, LISTS), BF16),
            pltpu.VMEM((ROWS, DEV * CAP), BF16),
            pltpu.VMEM((NP, 1, BLK), I32),
            pltpu.VMEM((NP, 1, BLK), I32),
            pltpu.VMEM((NL, NP, BLK), I32),
            pltpu.VMEM((NL, NP, BLK), I32),
            pltpu.SemaphoreType.DMA((2,)),
            pltpu.SemaphoreType.DMA((2,)),
            pltpu.SemaphoreType.DMA((4,)),
            pltpu.SemaphoreType.DMA((4,)),
            pltpu.SemaphoreType.REGULAR,
        ],
        compiler_params=pltpu.CompilerParams(
            collective_id=0, has_side_effects=True, vmem_limit_bytes=36 << 20
        ),
        cost_estimate=pl.CostEstimate(flops=14 << 30, bytes_accessed=10 << 20, transcendentals=0),
    )(*(pltpu.with_memory_space_constraint(a, pltpu.HBM) for a in arrays))
    return pl.pallas_call(
        finish,
        out_shape=(jax.ShapeDtypeStruct((ROWS, D), BF16), means),
        in_specs=[vmem, vmem, hbm],
        out_specs=(hbm, hbm),
        scratch_shapes=[pltpu.VMEM((ROWS, D), BF16), pltpu.SemaphoreType.DMA((2 * PARTS,))],
        compiler_params=pltpu.CompilerParams(vmem_limit_bytes=16 << 20),
        cost_estimate=pl.CostEstimate(flops=1 << 30, bytes_accessed=9 << 20, transcendentals=0),
    )(unpack, rows, cent)


def solution(mesh):
    split = P(("passage", "list"), None)
    return jax.shard_map(
        shards,
        mesh=mesh,
        in_specs=(split, P(("passage", "list")), split, P()),
        out_specs=(split, split),
        check_vma=False,
    )
```

```python
import random

import jax
import jax.numpy as jnp
from jax import lax
from jax.experimental import pallas as pl
from jax.experimental.pallas import tpu as pltpu
from jax.sharding import PartitionSpec as P

NP, NL = 8, 16
DEV = NP * NL
CAP = 8
ROWS = 512
LISTS = 512
D = 1024
BLK = NL * CAP
TILE = 256
PARTS = 4
PACK = 512
CHUNKS = (16, 16, 32, 32, 16, 16)
WIDE = 512
MESH = pl.DeviceIdType.MESH
F32, BF16, I32 = jnp.float32, jnp.bfloat16, jnp.int32


def dot(a, b):
    return jnp.dot(a, b, preferred_element_type=F32)


def iota(shape, dim):
    return lax.broadcasted_iota(I32, shape, dim)


def wrap(v, n):
    return jnp.where(v >= n, v - n, v)


def steps(offset):
    return sum(min(d, 4 - d) for d in offset)


def send_order(seed):
    offsets = [(a, b, c) for a in range(4) for b in range(4) for c in range(4)]
    random.Random(seed).shuffle(offsets)
    return sorted(offsets, key=steps, reverse=True)


OFFSETS = send_order(3)
CHIPS = len(OFFSETS)
HERE = (0, 0, 0)


def seen_from_there(offset):
    return OFFSETS.index(tuple((4 - d) % 4 for d in offset))


class Place:
    def __init__(self):
        self.p, self.l = lax.axis_index("passage"), lax.axis_index("list")
        x, self.y_hi = lax.div(self.l, 4), lax.div(self.p, 4)
        z, rest = self.p - 4 * self.y_hi, self.l - 4 * x
        self.y_lo = lax.div(rest, 2)
        self.core = rest - 2 * self.y_lo
        y = 2 * self.y_hi + self.y_lo
        ys = [wrap(y + d, 4) for d in range(4)]
        self.x_part = [4 * wrap(x + d, 4) for d in range(4)]
        self.z_part = [wrap(z + d, 4) for d in range(4)]
        self.hi_part = [jnp.where(v >= 2, 4, 0) for v in ys]
        self.lo_part = [2 * (v - jnp.where(v >= 2, 2, 0)) for v in ys]
        self.me = self.p * NL + self.l

    def at(self, offset, core):
        a, b, c = offset
        return (self.hi_part[b] + self.z_part[c], self.x_part[a] + self.lo_part[b] + core)


def whole(ref, sem):
    pltpu.make_async_copy(ref, ref, sem).wait()


def signal(sem, device):
    pl.semaphore_signal(sem, inc=1, device_id=device, device_id_type=MESH)


def kernel(
    ids_hbm, pass_hbm, old_hbm, rot_hbm, recv2, cent_out, unpack_out,
    ids_ref, pass_ref, old, rot, rot_hi, rot_lo, send1, recv1, send2,
    cent, cent_hi, cent_lo, res, member, member_t, unpack,
    id1_s, id1_r, id2_s, id2_r,
    sem_send, sem_recv, sem_id, sem_local, sem_bar,
):
    at = Place()
    p, l, me = at.p, at.l, at.me

    load_ids = pltpu.make_async_copy(ids_hbm, ids_ref, sem_local.at[0])
    load_pass = pltpu.make_async_copy(pass_hbm, pass_ref, sem_local.at[1])
    load_rot = pltpu.make_async_copy(rot_hbm, rot, sem_local.at[2])
    load_old = pltpu.make_async_copy(old_hbm, old, sem_local.at[3])
    load_ids.start()
    load_pass.start()

    barrier = pltpu.get_barrier_semaphore()
    plane = [(0, b, c) for b in (2, 1, 3, 0) for c in (2, 1, 3, 0) if (b, c) != (0, 0)]
    line = [(a, 0, 0) for a in (2, 1, 3)]
    for offset in plane:
        signal(barrier, at.at(offset, at.core))
    for offset in line:
        for core in range(2):
            signal(barrier, at.at(offset, core))
    signal(barrier, at.at(HERE, 1 - at.core))
    load_rot.start()
    load_old.start()

    load_ids.wait()
    ids_row = ids_ref[...].astype(F32)
    eye = iota((ROWS, ROWS), 0) == iota((ROWS, ROWS), 1)
    ids_col = jnp.sum(jnp.where(eye, ids_row, 0.0), axis=1, keepdims=True)
    own_row = jnp.floor(ids_row * (1.0 / LISTS))
    own_col = jnp.floor(ids_col * (1.0 / LISTS))
    before_row = jnp.sum(jnp.where(own_col < own_row, 1.0, 0.0), axis=0, keepdims=True)
    slot_row = (own_row * CAP + iota((1, ROWS), 1).astype(F32) - before_row).astype(I32)

    load_pass.wait()

    def fill(b, _):
        hit = slot_row == iota((PACK, ROWS), 0) + b * PACK
        hit = jnp.where(hit, 1.0, 0.0).astype(BF16)
        at_b = pl.ds(b * (PACK // CAP), PACK // CAP)
        for n in range(D // TILE):
            cols = slice(n * TILE, (n + 1) * TILE)
            send1[at_b, :, cols] = dot(hit, pass_ref[:, cols]).astype(BF16).reshape(PACK // CAP, CAP, TILE)
        return 0

    lax.fori_loop(0, DEV * CAP // PACK, fill, 0)

    def route(offset, core):
        device = at.at(offset, core)
        pltpu.make_async_remote_copy(
            src_ref=send1.at[device[0] * NL + device[1]], dst_ref=recv1.at[(1 - at.core) * CHIPS + seen_from_there(offset)],
            send_sem=sem_send.at[0], recv_sem=sem_recv.at[0], device_id=device, device_id_type=MESH,
        ).start()

    pl.semaphore_wait(barrier, len(plane) + 2 * len(line) + 1)
    for offset in plane:
        signal(sem_bar, at.at(offset, at.core))
    for offset in plane:
        route(offset, at.core)
    for offset in line:
        for core in range(2):
            route(offset, core)
    route(HERE, 1 - at.core)
    pltpu.make_async_copy(send1.at[me], recv1.at[(1 - at.core) * CHIPS + OFFSETS.index(HERE)], sem_recv.at[0]).start()

    before_col = jnp.sum(jnp.where(own_row < own_col, 1.0, 0.0), axis=1, keepdims=True)
    slot_col = (own_col * CAP + iota((ROWS, 1), 0).astype(F32) - before_col).astype(I32)
    mark_col = ids_col - own_col * LISTS + 1.0
    for b in range(NP):
        hit = slot_col == iota((ROWS, BLK), 1) + b * BLK
        id1_s[b] = jnp.sum(jnp.where(hit, mark_col, 0.0), axis=0, keepdims=True).astype(I32)
        unpack[:, b * BLK : (b + 1) * BLK] = jnp.where(hit, 1.0, 0.0).astype(BF16)
    for b in (2, 0):
        for c in (2, 1, 3, 0):
            if (b, c) != (0, 0):
                device = at.at((0, b, c), at.core)
                pltpu.make_async_remote_copy(
                    src_ref=id1_s.at[device[0]], dst_ref=id1_r.at[p], send_sem=sem_id.at[0], recv_sem=sem_id.at[1],
                    device_id=device, device_id_type=MESH,
                ).start()
    pltpu.make_async_copy(id1_s.at[p], id1_r.at[p], sem_id.at[1]).start()
    store_unpack = pltpu.make_async_copy(unpack, unpack_out, sem_local.at[0])
    store_unpack.start()
    pl.semaphore_wait(sem_bar, len(plane))

    others = [offset for offset in OFFSETS if offset[0] != 0 and offset[1:] != (0, 0)]

    def route_all(core):
        for offset in others:
            route(offset, core)

        @pl.when(at.core != core)
        def _():
            for offset in plane:
                route(offset, core)

    route_all(0)

    whole(id1_r, sem_id.at[1])
    source = iota((NP, BLK), 1) // CAP
    got = id1_r[...].reshape(NP, BLK)
    for k in range(NL):
        spread = jnp.where(source == k, got, 0)
        for turn in (CAP, 2 * CAP, 4 * CAP, 8 * CAP):
            spread = spread + pltpu.roll(spread, turn, 1)
        id2_s[k] = spread
    for k in range(1, NL):
        other = wrap(l + k, NL)
        pltpu.make_async_remote_copy(
            src_ref=id2_s.at[other], dst_ref=id2_r.at[l], send_sem=sem_id.at[2], recv_sem=sem_id.at[3],
            device_id=(p, other), device_id_type=MESH,
        ).start()
    pltpu.make_async_copy(id2_s.at[l], id2_r.at[l], sem_id.at[3]).start()

    route_all(1)

    load_rot.wait()

    def split_rot(i, _):
        s = pl.ds(pl.multiple_of(i * 128, 128), 128)
        full = rot[s, :]
        high = full.astype(BF16)
        rot_hi[s, :] = high
        rot_lo[s, :] = (full - high.astype(F32)).astype(BF16)
        return 0

    lax.fori_loop(0, D // 128, split_rot, 0)

    whole(id2_r, sem_id.at[3])
    row_of = jnp.zeros((CHIPS, 1), I32)
    for k, offset in enumerate(OFFSETS):
        there_p, there_l = at.at(offset, 0)
        row_of = jnp.where(iota((CHIPS, 1), 0) == k, there_l * NP + there_p, row_of)
    here = iota((CHIPS, DEV), 1)
    order = jnp.concatenate([here == row_of + NP, here == row_of], axis=0)
    order = jnp.where(order, 1.0, 0.0).astype(BF16)
    marks = id2_r[...].reshape(DEV, BLK).astype(F32)
    high = jnp.floor(marks * (1.0 / 16))
    marks = dot(order, high.astype(BF16)) * 16.0 + dot(order, (marks - high * 16.0).astype(BF16))
    marks = jnp.where(iota((DEV, BLK), 0) % NL == iota((DEV, BLK), 1) // CAP, marks, 0.0)
    eye = iota((BLK, BLK), 0) == iota((BLK, BLK), 1)
    tally = jnp.zeros((LISTS, 1), F32)
    for b in range(NP):
        row = jnp.sum(marks[b * NL : (b + 1) * NL, :], axis=0, keepdims=True)
        hit = jnp.where(iota((LISTS, BLK), 0) + 1 == row.astype(I32), 1.0, 0.0)
        member[:, b * BLK : (b + 1) * BLK] = hit.astype(BF16)
        tally = tally + jnp.sum(hit, axis=1, keepdims=True)
        col = jnp.sum(jnp.where(eye, row, 0.0), axis=1, keepdims=True).astype(I32)
        hit = jnp.where(iota((BLK, LISTS), 1) + 1 == col, 1.0, 0.0)
        member_t[b * BLK : (b + 1) * BLK, :] = hit.astype(BF16)
    load_old.wait()
    tally = tally + 1.0

    whole(recv1, sem_recv.at[0])
    for n in range(D // TILE):
        s = slice(n * TILE, (n + 1) * TILE)
        sums = dot(member[...], recv1[:, :, s].reshape(DEV * CAP, TILE))
        mean = (sums + old[:, s]) / tally
        high = mean.astype(BF16)
        cent[:, s] = mean
        cent_hi[:, s] = high
        cent_lo[:, s] = (mean - high.astype(F32)).astype(BF16)
    store_cent = pltpu.make_async_copy(cent, cent_out, sem_local.at[1])
    store_cent.start()

    first = 0
    for count in CHUNKS:
        here = slice(first, first + count)
        rows = count * CAP
        pick = member_t[first * CAP : first * CAP + rows, :]
        for n in range(D // WIDE):
            s = slice(n * WIDE, (n + 1) * WIDE)
            near = dot(pick, cent_hi[:, s]) + dot(pick, cent_lo[:, s])
            part = recv1[here, :, s].reshape(rows, WIDE).astype(F32) - near
            high = part.astype(BF16)
            res[:rows, s] = high
            res[rows : 2 * rows, s] = (part - high.astype(F32)).astype(BF16)
        for n in range(D // WIDE):
            s = slice(n * WIDE, (n + 1) * WIDE)
            both = dot(res[: 2 * rows], rot_hi[:, s])
            turned = both[:rows] + both[rows:] + dot(res[:rows], rot_lo[:, s])
            send2[here, :, s] = turned.astype(BF16).reshape(count, CAP, WIDE)

        for k in range(first, first + count):
            core, offset = 1 - k // CHIPS, OFFSETS[k % CHIPS]

            def give_back():
                pltpu.make_async_remote_copy(
                    src_ref=send2.at[k], dst_ref=recv2.at[me], send_sem=sem_send.at[1], recv_sem=sem_recv.at[1],
                    device_id=at.at(offset, core), device_id_type=MESH,
                ).start()

            if offset == HERE:
                pl.when(at.core != core)(give_back)
            else:
                give_back()
        first += count

    mine = send2.at[(1 - at.core) * CHIPS + OFFSETS.index(HERE)]
    pltpu.make_async_copy(mine, recv2.at[me], sem_recv.at[1]).start()

    whole(send1.at[pl.ds(0, DEV - 1)], sem_send.at[0])
    whole(id1_s.at[pl.ds(0, NP - 1)], sem_id.at[0])
    whole(id2_s.at[pl.ds(0, NL - 1)], sem_id.at[2])
    store_unpack.wait()
    store_cent.wait()
    whole(send2.at[pl.ds(0, DEV - 1)], sem_send.at[1])
    whole(recv2, sem_recv.at[1])


def finish(unpack, rows, cent, out, cent_out, buf, sem):
    stores = []

    def store(src, dst):
        stores.append(pltpu.make_async_copy(src, dst, sem.at[len(stores)]))
        stores[-1].start()

    for n in range(PARTS):
        rows_n = pl.ds(n * (LISTS // PARTS), LISTS // PARTS)
        store(cent.at[rows_n], cent_out.at[rows_n])
    for n in range(PARTS):
        rows_n = pl.ds(n * (ROWS // PARTS), ROWS // PARTS)
        buf[rows_n] = dot(unpack[rows_n], rows[...].reshape(DEV * CAP, D)).astype(BF16)
        store(buf.at[rows_n], out.at[rows_n])
    for copy in stores:
        copy.wait()


def shards(passages, list_ids, old_centroids, rotation):
    vmem = pl.BlockSpec(memory_space=pltpu.VMEM)
    hbm = pl.BlockSpec(memory_space=pl.ANY)
    slots = jax.ShapeDtypeStruct((DEV, CAP, D), BF16)
    buffer = pltpu.VMEM((DEV, CAP, D), BF16)
    means = jax.ShapeDtypeStruct((LISTS, D), F32)
    arrays = (list_ids.reshape(1, ROWS), passages, old_centroids, rotation)
    rows, cent, unpack = pl.pallas_call(
        kernel,
        out_shape=(slots, means, jax.ShapeDtypeStruct((ROWS, DEV * CAP), BF16)),
        in_specs=[hbm] * 4,
        out_specs=(hbm,) * 3,
        scratch_shapes=[
            pltpu.VMEM((1, ROWS), I32),
            pltpu.VMEM((ROWS, D), BF16),
            pltpu.VMEM((LISTS, D), F32),
            pltpu.VMEM((D, D), F32),
            pltpu.VMEM((D, D), BF16),
            pltpu.VMEM((D, D), BF16),
            buffer, buffer, buffer,
            pltpu.VMEM((LISTS, D), F32),
            pltpu.VMEM((LISTS, D), BF16),
            pltpu.VMEM((LISTS, D), BF16),
            pltpu.VMEM((2 * max(CHUNKS) * CAP, D), BF16),
            pltpu.VMEM((LISTS, DEV * CAP), BF16),
            pltpu.VMEM((DEV * CAP, LISTS), BF16),
            pltpu.VMEM((ROWS, DEV * CAP), BF16),
            pltpu.VMEM((NP, 1, BLK), I32),
            pltpu.VMEM((NP, 1, BLK), I32),
            pltpu.VMEM((NL, NP, BLK), I32),
            pltpu.VMEM((NL, NP, BLK), I32),
            pltpu.SemaphoreType.DMA((2,)),
            pltpu.SemaphoreType.DMA((2,)),
            pltpu.SemaphoreType.DMA((4,)),
            pltpu.SemaphoreType.DMA((4,)),
            pltpu.SemaphoreType.REGULAR,
        ],
        compiler_params=pltpu.CompilerParams(
            collective_id=0, has_side_effects=True, vmem_limit_bytes=36 << 20
        ),
        cost_estimate=pl.CostEstimate(flops=14 << 30, bytes_accessed=10 << 20, transcendentals=0),
    )(*(pltpu.with_memory_space_constraint(a, pltpu.HBM) for a in arrays))
    return pl.pallas_call(
        finish,
        out_shape=(jax.ShapeDtypeStruct((ROWS, D), BF16), means),
        in_specs=[vmem, vmem, hbm],
        out_specs=(hbm, hbm),
        scratch_shapes=[pltpu.VMEM((ROWS, D), BF16), pltpu.SemaphoreType.DMA((2 * PARTS,))],
        compiler_params=pltpu.CompilerParams(vmem_limit_bytes=16 << 20),
        cost_estimate=pl.CostEstimate(flops=1 << 30, bytes_accessed=9 << 20, transcendentals=0),
    )(unpack, rows, cent)


def solution(mesh):
    split = P(("passage", "list"), None)
    return jax.shard_map(
        shards,
        mesh=mesh,
        in_specs=(split, P(("passage", "list")), split, P()),
        out_specs=(split, split),
        check_vma=False,
    )
```
